256 devices in a mesh: seq: 64 (over z, x, core), head: 4 (over y).
Axes of the slice: x: 4, y: 4, z: 8, core: 2. Of those that a mesh axis runs over, the one named last changes fastest.
Arguments:
- queries: bfloat16 [32768, 4096], P(('seq', 'head')), may hold values from -6 to 6
- keys: bfloat16 [32768, 4096], P(('seq', 'head')), may hold values from -6 to 6
- values: bfloat16 [32768, 4096], P(('seq', 'head')), may hold values from -6 to 6
- grad_out: bfloat16 [32768, 4096], P(('seq', 'head')), may hold values from -0.0029296875 to 0.0029296875
Outputs:
- grad_queries: bfloat16 [32768, 4096], P(('seq', 'head'))
- grad_keys: bfloat16 [32768, 4096], P(('seq', 'head'))
- grad_values: bfloat16 [32768, 4096], P(('seq', 'head'))
The draws below stay inside these ranges and needn't reach their ends.
All inputs are finite; a program needn't handle non-finite values.
Results may differ from the reference program's by a relative error of at most 0.005.
Values may be sent and summed in bfloat16 or wider, within the bound.
A program may use at most 256 MiB of HBM per device.

```python
import jax
import jax.numpy as jnp
from jax import lax

H = 32
DH = 128
BLOCK = 512
TOKENS = 32768


def steps_of(stream_key, extent, cuts, least, top_value):
    def one(dim, blocks):
        draws = jax.random.uniform(jax.random.fold_in(jax.random.fold_in(stream_key, 6), dim), (blocks,), jnp.float32, least / len(cuts), top_value / len(cuts))
        return jnp.repeat(jnp.exp(draws), extent[dim] // blocks).reshape((-1,) + (1,) * (len(extent) - dim - 1))

    factor_of = one(*cuts[0])
    for cut in cuts[1:]:
        factor_of = factor_of * one(*cut)
    return factor_of


def noise(rng, dims, deviation, most, shards=(), held_as=jnp.bfloat16):
    factor_of = steps_of(rng, dims, shards, -0.22, 0.18) if shards else 1.0
    drawn = jax.random.normal(rng, dims, jnp.float32) * deviation * factor_of
    return jnp.minimum(jnp.maximum(drawn, -most), most).astype(held_as)


def setup_inputs(seed: int = 0) -> dict:
    streams_of = jax.random.split(jax.random.key(seed), 5)
    return {
        "queries": noise(streams_of[0], (TOKENS, H * DH), 1.0, 6.0, ((0, 256),)),
        "keys": noise(streams_of[1], (TOKENS, H * DH), 1.0, 6.0, ((0, 256),)),
        "values": noise(streams_of[2], (TOKENS, H * DH), 1.0, 6.0, ((0, 256),)),
        "grad_out": noise(streams_of[3], (TOKENS, H * DH), (DH * TOKENS) ** -0.5, 0.0029296875, ((0, 256),)),
    }


def widen(array):
    return array.astype(jnp.float32)


def block_states(pieces):
    queries, keys, values, grads = pieces
    key_state = jnp.einsum('shd,she->hde', widen(keys), widen(values))
    grad_state = jnp.einsum('thd,the->hde', widen(queries), widen(grads))
    return key_state, grad_state


def block_grads(pieces):
    queries, keys, values, grads, prefix, suffix = pieces
    length = queries.shape[0]
    row_index = lax.broadcasted_iota(jnp.int32, (length, length), 0)
    column_index = lax.broadcasted_iota(jnp.int32, (length, length), 1)
    causal = (column_index <= row_index)[None]
    grad_scores = jnp.where(causal, jnp.einsum('thd,shd->hts', widen(grads), widen(values)), 0.0).astype(jnp.bfloat16)
    query_scores = jnp.where(causal, jnp.einsum('thd,shd->hts', widen(queries), widen(keys)), 0.0).astype(jnp.bfloat16)
    grad_queries = jnp.einsum('hts,shd->thd', widen(grad_scores), widen(keys)) + jnp.einsum('the,hde->thd', widen(grads), widen(prefix))
    grad_keys = jnp.einsum('hts,thd->shd', widen(grad_scores), widen(queries)) + jnp.einsum('she,hde->shd', widen(values), widen(suffix))
    grad_values = jnp.einsum('hts,thd->shd', widen(query_scores), widen(grads)) + jnp.einsum('shd,hde->she', widen(keys), widen(suffix))
    return grad_queries.astype(jnp.bfloat16), grad_keys.astype(jnp.bfloat16), grad_values.astype(jnp.bfloat16)


def reference(queries, keys, values, grad_out):
    number = TOKENS // BLOCK
    shaped_queries = queries.reshape(number, BLOCK, H, DH)
    shaped_keys = keys.reshape(number, BLOCK, H, DH)
    shaped_values = values.reshape(number, BLOCK, H, DH)
    shaped_grads = grad_out.reshape(number, BLOCK, H, DH)
    key_state, grad_state = lax.map(block_states, (shaped_queries, shaped_keys, shaped_values, shaped_grads))
    empty_state = jnp.zeros_like(key_state[:1])
    prefix = jnp.concatenate([empty_state, jnp.cumsum(key_state, axis=0)[:-1]], axis=0).astype(jnp.bfloat16)
    suffix = jnp.concatenate([jnp.cumsum(grad_state[::-1], axis=0)[::-1][1:], empty_state], axis=0).astype(jnp.bfloat16)
    grad_queries, grad_keys, grad_values = lax.map(block_grads, (shaped_queries, shaped_keys, shaped_values, shaped_grads, prefix, suffix))
    return (grad_queries.reshape(TOKENS, H * DH), grad_keys.reshape(TOKENS, H * DH), grad_values.reshape(TOKENS, H * DH))
```

```python
import jax
import jax.numpy as jnp
from jax import lax
from jax.experimental import pallas as pl
from jax.experimental.pallas import tpu as pltpu
from jax.sharding import PartitionSpec as P

H = 32
DH = 128
NZ, NX, NY = 8, 4, 4
PER = H // NY
M = 4
HC = PER // M
R = HC * DH
RX = R // NX
MESH = pl.DeviceIdType.MESH
F32 = jnp.float32
BF16 = jnp.bfloat16


def dot(left, right, left_dim, right_dim):
    return lax.dot_general(
        left, right, (((left_dim,), (right_dim,)), ((), ())), preferred_element_type=F32
    )


def kernel(
    q_ref, k_ref, v_ref, g_ref, oq_ref, ok_ref, ov_ref,
    sent, got, own_total, other_total, core_out, x_out, x_in, z_buf, x_back, base, base_out, base_other,
    y_out, final, part_q, part_k, part_v,
    yi_s, yi_r, c1_s, c1_r, xi_s, xi_r, zz_s, zz_r, xo_s, xo_r, c2_s, c2_r, yo_s, yo_r,
):
    s = lax.axis_index("seq")
    y = lax.axis_index("head")
    c = lax.rem(s, 2)
    x = lax.rem(s // 2, NX)
    z = s // (2 * NX)
    forward = c == 0
    mate = (s + 1 - 2 * c, y)

    def at_y(d):
        return lax.rem(y + d, NY)

    def at_x(d):
        return lax.rem(x + d, NX)

    def at_z(d):
        return lax.rem(z + d, NZ)

    def x_dev(i):
        return ((z * NX + i) * 2 + c, y)

    def z_dev(i):
        return ((i * NX + x) * 2 + c, y)

    def copy(src, dst, send, recv, device):
        return pltpu.make_async_remote_copy(
            src_ref=src, dst_ref=dst, send_sem=send, recv_sem=recv, device_id=device, device_id_type=MESH
        )

    barrier = pltpu.get_barrier_semaphore()
    partners = (
        [mate]
        + [(s, at_y(d)) for d in range(1, NY)]
        + [x_dev(at_x(d)) for d in range(1, NX)]
        + [z_dev(at_z(d)) for d in range(1, NZ)]
    )
    for partner in partners:
        pl.semaphore_signal(barrier, inc=1, device_id=partner, device_id_type=MESH)

    def lanes(head):
        return pl.ds(pl.multiple_of(head * DH, DH), DH)

    def y_in(m, d, receive=False):
        slot = at_y(NY - d) if receive else y
        return copy(sent.at[m, at_y(d)], got.at[m, slot], yi_s.at[m, d], yi_r.at[m, d], (s, at_y(d)))

    def core_in(m):
        return copy(core_out.at[m], other_total.at[m], c1_s.at[m], c1_r.at[m], mate)

    def x_in_copy(m, d, receive=False):
        slot = at_x(NX - d) if receive else x
        return copy(x_out.at[m, at_x(d)], x_in.at[m, slot], xi_s.at[m, d], xi_r.at[m, d], x_dev(at_x(d)))

    def z_copy(m, d, receive=False):
        slot = at_z(NZ - d) if receive else z
        return copy(z_buf.at[m, z], z_buf.at[m, slot], zz_s.at[m, d], zz_r.at[m, d], z_dev(at_z(d)))

    def x_out_copy(m, d, receive=False):
        slot = at_x(NX - d) if receive else x
        return copy(x_back.at[m, at_x(d)], base.at[m, slot], xo_s.at[m, d], xo_r.at[m, d], x_dev(at_x(d)))

    def core_out_copy(m):
        return copy(base_out.at[m], base_other.at[m], c2_s.at[m], c2_r.at[m], mate)

    def y_out_copy(m, d, receive=False):
        slot = at_y(NY - d) if receive else y
        return copy(y_out.at[m, at_y(d)], final.at[m, slot], yo_s.at[m, d], yo_r.at[m, d], (s, at_y(d)))

    def states(m):
        for d in (2, 1, 3, 0):
            owner = at_y(d)

            @pl.loop(0, HC)
            def _(i):
                at = lanes(owner * PER + m * HC + i)
                rows = pl.ds(pl.multiple_of(i * DH, DH), DH)
                key_state = dot(k_ref[:, at], v_ref[:, at], 0, 0).astype(BF16)
                grad_state = dot(q_ref[:, at], g_ref[:, at], 0, 0).astype(BF16)
                if d:
                    sent[m, owner, 0, rows, :] = key_state
                    sent[m, owner, 1, rows, :] = grad_state
                else:
                    got[m, y, 0, rows, :] = key_state
                    got[m, y, 1, rows, :] = grad_state

            if d:
                y_in(m, d).start()

    def inside(m):
        row = lax.broadcasted_iota(jnp.int32, (DH, DH), 0)
        column = lax.broadcasted_iota(jnp.int32, (DH, DH), 1)
        causal = column <= row

        @pl.loop(0, NY * HC)
        def _(n):
            at = lanes(n // HC * PER + m * HC + lax.rem(n, HC))
            q, k, v, g = q_ref[:, at], k_ref[:, at], v_ref[:, at], g_ref[:, at]
            grad_scores = jnp.where(causal, dot(g, v, 1, 1), 0.0).astype(BF16)
            query_scores = jnp.where(causal, dot(q, k, 1, 1), 0.0).astype(BF16)
            part_q[:, at] = dot(grad_scores, k, 1, 0)
            part_k[:, at] = dot(grad_scores, q, 0, 0)
            part_v[:, at] = dot(query_scores, g, 0, 0)

    def stage_c(m):
        for d in range(1, NY):
            y_in(m, d, True).wait_recv()

        @pl.loop(0, HC)
        def _(i):
            rows = pl.ds(pl.multiple_of(i * DH, DH), DH)
            totals = []
            for kind in range(2):
                total = got[m, 0, kind, rows, :].astype(F32)
                for j in range(1, NY):
                    total += got[m, j, kind, rows, :].astype(F32)
                totals.append(total)
            own_total[m, rows, :] = jnp.where(forward, totals[0], totals[1])
            core_out[m, rows, :] = jnp.where(forward, totals[1], totals[0])

        core_in(m).start()

    def stage_d(m):
        core_in(m).wait_recv()
        for i in range(NX):
            rows = slice(i * RX, (i + 1) * RX)
            x_out[m, i] = own_total[m, rows, :] + other_total[m, rows, :]
        for d in range(1, NX):
            x_in_copy(m, d).start()
        x_in[m, x] = x_out[m, x]

    def stage_e(m):
        for d in range(1, NX):
            x_in_copy(m, d, True).wait_recv()
        total = x_in[m, 0]
        for i in range(1, NX):
            total += x_in[m, i]
        z_buf[m, z] = total.astype(BF16)
        for d in range(1, NZ):
            z_copy(m, d).start()

    def stage_z(m):
        for d in range(1, NZ):
            z_copy(m, d, True).wait_recv()
        before = jnp.zeros((RX, DH), F32)
        for i in range(NZ):
            wanted = jnp.where(forward, i < z, i > z)
            before += jnp.where(wanted, z_buf[m, i].astype(F32), 0.0)
        ahead = [before]
        behind = [before]
        for i in range(NX - 1):
            ahead.append(ahead[-1] + x_in[m, i])
            behind.append(behind[-1] + x_in[m, NX - 1 - i])
        for i in range(NX):
            x_back[m, i] = jnp.where(forward, ahead[i], behind[NX - 1 - i])
        for d in range(1, NX):
            x_out_copy(m, d).start()
        base[m, x] = x_back[m, x]

    def stage_f(m):
        for d in range(1, NX):
            x_out_copy(m, d, True).wait_recv()
        for i in range(NX):
            rows = slice(i * RX, (i + 1) * RX)
            base_out[m, rows, :] = base[m, i] + own_total[m, rows, :]
        core_out_copy(m).start()

    def stage_g(m):
        core_out_copy(m).wait_recv()
        for i in range(NX):
            rows = slice(i * RX, (i + 1) * RX)
            mine = base[m, i]
            theirs = base_other[m, rows, :]
            run = jnp.where(forward, mine, theirs)
            for j in range(NY):
                y_out[m, j, 0, rows, :] = run.astype(BF16)
                if j < NY - 1:
                    run += got[m, j, 0, rows, :].astype(F32)
            run = jnp.where(forward, theirs, mine)
            for j in range(NY - 1, -1, -1):
                y_out[m, j, 1, rows, :] = run.astype(BF16)
                if j:
                    run += got[m, j, 1, rows, :].astype(F32)
        for d in (2, 1, 3):
            y_out_copy(m, d).start()
        final[m, y] = y_out[m, y]

    def stage_h(m):
        for d in range(1, NY):
            y_out_copy(m, d, True).wait_recv()

        @pl.loop(0, NY * HC)
        def _(n):
            owner, i = n // HC, lax.rem(n, HC)
            at = lanes(owner * PER + m * HC + i)
            rows = pl.ds(pl.multiple_of(i * DH, DH), DH)
            prefix = final[m, owner, 0, rows, :]
            suffix = final[m, owner, 1, rows, :]
            oq_ref[:, at] = (part_q[:, at] + dot(g_ref[:, at], prefix, 1, 1)).astype(BF16)
            ok_ref[:, at] = (part_k[:, at] + dot(v_ref[:, at], suffix, 1, 1)).astype(BF16)
            ov_ref[:, at] = (part_v[:, at] + dot(k_ref[:, at], suffix, 1, 0)).astype(BF16)

    pl.semaphore_wait(barrier, len(partners))
    for m in range(M):
        states(m)
    for m in range(M):
        inside(m)
    stage_c(0)
    stage_d(0)
    stage_e(0)
    for m in range(M):
        stage_z(m)
        if m + 1 < M:
            stage_c(m + 1)
        stage_f(m)
        if m + 1 < M:
            stage_d(m + 1)
        stage_g(m)
        if m + 1 < M:
            stage_e(m + 1)
    for m in range(M):
        stage_h(m)
    for m in range(M):
        for d in range(1, NY):
            y_in(m, d).wait_send()
            y_out_copy(m, d).wait_send()
        for d in range(1, NX):
            x_in_copy(m, d).wait_send()
            x_out_copy(m, d).wait_send()
        for d in range(1, NZ):
            z_copy(m, d).wait_send()
        core_in(m).wait_send()
        core_out_copy(m).wait_send()


def shards(queries, keys, values, grad_out):
    tokens = queries.shape[0]
    whole = pl.BlockSpec(memory_space=pltpu.VMEM)
    dma = pltpu.SemaphoreType.DMA
    return pl.pallas_call(
        kernel,
        out_shape=[jax.ShapeDtypeStruct((tokens, H * DH), BF16)] * 3,
        in_specs=[whole] * 4,
        out_specs=[whole] * 3,
        scratch_shapes=[
            pltpu.VMEM((M, NY, 2, R, DH), BF16),
            pltpu.VMEM((M, NY, 2, R, DH), BF16),
            pltpu.VMEM((M, R, DH), F32),
            pltpu.VMEM((M, R, DH), F32),
            pltpu.VMEM((M, R, DH), F32),
            pltpu.VMEM((M, NX, RX, DH), F32),
            pltpu.VMEM((M, NX, RX, DH), F32),
            pltpu.VMEM((M, NZ, RX, DH), BF16),
            pltpu.VMEM((M, NX, RX, DH), F32),
            pltpu.VMEM((M, NX, RX, DH), F32),
            pltpu.VMEM((M, R, DH), F32),
            pltpu.VMEM((M, R, DH), F32),
            pltpu.VMEM((M, NY, 2, R, DH), BF16),
            pltpu.VMEM((M, NY, 2, R, DH), BF16),
            pltpu.VMEM((tokens, H * DH), F32),
            pltpu.VMEM((tokens, H * DH), F32),
            pltpu.VMEM((tokens, H * DH), F32),
            dma((M, NY)), dma((M, NY)),
            dma((M,)), dma((M,)),
            dma((M, NX)), dma((M, NX)),
            dma((M, NZ)), dma((M, NZ)),
            dma((M, NX)), dma((M, NX)),
            dma((M,)), dma((M,)),
            dma((M, NY)), dma((M, NY)),
        ],
        compiler_params=pltpu.CompilerParams(
            collective_id=0, has_side_effects=True, vmem_limit_bytes=48 * 2**20
        ),
        cost_estimate=pl.CostEstimate(
            flops=20 * DH**3 * H, bytes_accessed=14 * tokens * H * DH, transcendentals=0
        ),
        name="scan",
    )(queries, keys, values, grad_out)


def solution(mesh):
    spec = P(("seq", "head"), None)
    return jax.shard_map(
        shards, mesh=mesh, in_specs=(spec,) * 4, out_specs=(spec,) * 3, check_vma=False
    )
```

```python
import jax
import jax.numpy as jnp
from jax import lax
from jax.experimental import pallas as pl
from jax.experimental.pallas import tpu as pltpu
from jax.sharding import PartitionSpec as P

H = 32
DH = 128
NZ, NX, NY = 8, 4, 4
PER = H // NY
M = 4
HC = PER // M
WIDE = NY * HC * DH
R = HC * DH
RX = R // NX
UNROLL = 4
MESH = pl.DeviceIdType.MESH
F32 = jnp.float32
BF16 = jnp.bfloat16


def dot(left, right, left_dim, right_dim):
    return lax.dot_general(
        left, right, (((left_dim,), (right_dim,)), ((), ())), preferred_element_type=F32
    )


def kernel(
    q_hbm, k_hbm, v_hbm, g_hbm, oq_hbm, ok_hbm, ov_hbm,
    q_ref, k_ref, v_ref, g_ref, oq_ref, ok_ref, ov_ref, sent, got, own_total, other_total, core_out, x_out, x_in, z_buf, x_back, base, base_out, base_other,
    y_out, final, part_q, part_k, part_v,
    in_sem, out_sem, yi_s, yi_r, c1_s, c1_r, xi_s, xi_r, zz_s, zz_r, xo_s, xo_r, c2_s, c2_r, yo_s, yo_r,
):
    s = lax.axis_index("seq")
    y = lax.axis_index("head")
    c = lax.rem(s, 2)
    x = lax.rem(s // 2, NX)
    z = s // (2 * NX)
    forward = c == 0
    mate = (s + 1 - 2 * c, y)

    def at_y(d):
        return lax.rem(y + d, NY)

    def at_x(d):
        return lax.rem(x + d, NX)

    def at_z(d):
        return lax.rem(z + d, NZ)

    def x_dev(i):
        return ((z * NX + i) * 2 + c, y)

    def z_dev(i):
        return ((i * NX + x) * 2 + c, y)

    def copy(src, dst, send, recv, device):
        return pltpu.make_async_remote_copy(
            src_ref=src, dst_ref=dst, send_sem=send, recv_sem=recv, device_id=device, device_id_type=MESH
        )

    barrier = pltpu.get_barrier_semaphore()
    partners = (
        [mate]
        + [(s, at_y(d)) for d in range(1, NY)]
        + [x_dev(at_x(d)) for d in range(1, NX)]
        + [z_dev(at_z(d)) for d in range(1, NZ)]
    )
    for partner in partners:
        pl.semaphore_signal(barrier, inc=1, device_id=partner, device_id_type=MESH)

    def lanes(m, owner, i):
        return pl.ds(pl.multiple_of(((m * NY + owner) * HC + i) * DH, DH), DH)

    def load(m):
        columns = slice(m * WIDE, (m + 1) * WIDE)
        pairs = ((k_hbm, k_ref), (v_hbm, v_ref), (q_hbm, q_ref), (g_hbm, g_ref))
        return [
            pltpu.make_async_copy(a.at[:, columns], b.at[:, columns], in_sem.at[m, n])
            for n, (a, b) in enumerate(pairs)
        ]

    def store(m):
        columns = slice(m * WIDE, (m + 1) * WIDE)
        pairs = ((oq_ref, oq_hbm), (ok_ref, ok_hbm), (ov_ref, ov_hbm))
        return [
            pltpu.make_async_copy(a.at[:, columns], b.at[:, columns], out_sem.at[m, n])
            for n, (a, b) in enumerate(pairs)
        ]

    for m in range(M):
        for one in load(m):
            one.start()

    def y_in(m, d, receive=False):
        slot = at_y(NY - d) if receive else y
        return copy(sent.at[m, at_y(d)], got.at[m, slot], yi_s.at[m, d], yi_r.at[m, d], (s, at_y(d)))

    def core_in(m):
        return copy(core_out.at[m], other_total.at[m], c1_s.at[m], c1_r.at[m], mate)

    def x_in_copy(m, d, receive=False):
        slot = at_x(NX - d) if receive else x
        return copy(x_out.at[m, at_x(d)], x_in.at[m, slot], xi_s.at[m, d], xi_r.at[m, d], x_dev(at_x(d)))

    def z_copy(m, d, receive=False):
        slot = at_z(NZ - d) if receive else z
        return copy(z_buf.at[m, z], z_buf.at[m, slot], zz_s.at[m, d], zz_r.at[m, d], z_dev(at_z(d)))

    def x_out_copy(m, d, receive=False):
        slot = at_x(NX - d) if receive else x
        return copy(x_back.at[m, at_x(d)], base.at[m, slot], xo_s.at[m, d], xo_r.at[m, d], x_dev(at_x(d)))

    def core_out_copy(m):
        return copy(base_out.at[m], base_other.at[m], c2_s.at[m], c2_r.at[m], mate)

    def y_out_copy(m, d, receive=False):
        slot = at_y(NY - d) if receive else y
        return copy(y_out.at[m, at_y(d)], final.at[m, slot], yo_s.at[m, d], yo_r.at[m, d], (s, at_y(d)))

    def states(m):
        for one in load(m):
            one.wait()
        for d in (2, 1, 3, 0):
            owner = at_y(d)
            for i in range(HC):
                at = lanes(m, owner, i)
                rows = slice(i * DH, (i + 1) * DH)
                key_state = dot(k_ref[:, at], v_ref[:, at], 0, 0).astype(BF16)
                grad_state = dot(q_ref[:, at], g_ref[:, at], 0, 0).astype(BF16)
                if d:
                    sent[m, owner, 0, rows, :] = key_state
                    sent[m, owner, 1, rows, :] = grad_state
                else:
                    got[m, y, 0, rows, :] = key_state
                    got[m, y, 1, rows, :] = grad_state
            if d:
                y_in(m, d).start()

    def inside(m):
        row = lax.broadcasted_iota(jnp.int32, (DH, DH), 0)
        column = lax.broadcasted_iota(jnp.int32, (DH, DH), 1)
        causal = column <= row

        @pl.loop(0, NY * HC // UNROLL)
        def _(n):
            for u in range(UNROLL):
                at = lanes(m, 0, n * UNROLL + u)
                q, k, v, g = q_ref[:, at], k_ref[:, at], v_ref[:, at], g_ref[:, at]
                grad_scores = jnp.where(causal, dot(g, v, 1, 1), 0.0).astype(BF16)
                query_scores = jnp.where(causal, dot(q, k, 1, 1), 0.0).astype(BF16)
                part_q[:, at] = dot(grad_scores, k, 1, 0)
                part_k[:, at] = dot(grad_scores, q, 0, 0)
                part_v[:, at] = dot(query_scores, g, 0, 0)

    def stage_c(m):
        for d in range(1, NY):
            y_in(m, d, True).wait_recv()

        @pl.loop(0, HC)
        def _(i):
            rows = pl.ds(pl.multiple_of(i * DH, DH), DH)
            totals = []
            for kind in range(2):
                total = got[m, 0, kind, rows, :].astype(F32)
                for j in range(1, NY):
                    total += got[m, j, kind, rows, :].astype(F32)
                totals.append(total)
            own_total[m, rows, :] = jnp.where(forward, totals[0], totals[1])
            core_out[m, rows, :] = jnp.where(forward, totals[1], totals[0])

        core_in(m).start()

    def stage_d(m):
        core_in(m).wait_recv()
        for i in range(NX):
            rows = slice(i * RX, (i + 1) * RX)
            x_out[m, i] = own_total[m, rows, :] + other_total[m, rows, :]
        for d in range(1, NX):
            x_in_copy(m, d).start()
        x_in[m, x] = x_out[m, x]

    def stage_e(m):
        for d in range(1, NX):
            x_in_copy(m, d, True).wait_recv()
        total = x_in[m, 0]
        for i in range(1, NX):
            total += x_in[m, i]
        z_buf[m, z] = total.astype(BF16)
        for d in range(1, NZ):
            z_copy(m, d).start()

    def stage_z(m):
        for d in range(1, NZ):
            z_copy(m, d, True).wait_recv()
        before = jnp.zeros((RX, DH), F32)
        for i in range(NZ):
            wanted = jnp.where(forward, i < z, i > z)
            before += jnp.where(wanted, z_buf[m, i].astype(F32), 0.0)
        ahead = [before]
        behind = [before]
        for i in range(NX - 1):
            ahead.append(ahead[-1] + x_in[m, i])
            behind.append(behind[-1] + x_in[m, NX - 1 - i])
        for i in range(NX):
            x_back[m, i] = jnp.where(forward, ahead[i], behind[NX - 1 - i])
        for d in range(1, NX):
            x_out_copy(m, d).start()
        base[m, x] = x_back[m, x]

    def stage_f(m):
        for d in range(1, NX):
            x_out_copy(m, d, True).wait_recv()
        for i in range(NX):
            rows = slice(i * RX, (i + 1) * RX)
            base_out[m, rows, :] = base[m, i] + own_total[m, rows, :]
        core_out_copy(m).start()

    def stage_g(m):
        core_out_copy(m).wait_recv()
        for i in range(NX):
            rows = slice(i * RX, (i + 1) * RX)
            mine = base[m, i]
            theirs = base_other[m, rows, :]
            run = jnp.where(forward, mine, theirs)
            for j in range(NY):
                y_out[m, j, 0, rows, :] = run.astype(BF16)
                if j < NY - 1:
                    run += got[m, j, 0, rows, :].astype(F32)
            run = jnp.where(forward, theirs, mine)
            for j in range(NY - 1, -1, -1):
                y_out[m, j, 1, rows, :] = run.astype(BF16)
                if j:
                    run += got[m, j, 1, rows, :].astype(F32)
        for d in (2, 1, 3):
            y_out_copy(m, d).start()
        final[m, y] = y_out[m, y]

    def stage_h(m):
        for d in range(1, NY):
            y_out_copy(m, d, True).wait_recv()

        @pl.loop(0, NY * HC // UNROLL)
        def _(n):
            for u in range(UNROLL):
                owner, i = (n * UNROLL + u) // HC, lax.rem(n * UNROLL + u, HC)
                at = lanes(m, owner, i)
                rows = pl.ds(pl.multiple_of(i * DH, DH), DH)
                prefix = final[m, owner, 0, rows, :]
                suffix = final[m, owner, 1, rows, :]
                oq_ref[:, at] = (part_q[:, at] + dot(g_ref[:, at], prefix, 1, 1)).astype(BF16)
                ok_ref[:, at] = (part_k[:, at] + dot(v_ref[:, at], suffix, 1, 1)).astype(BF16)
                ov_ref[:, at] = (part_v[:, at] + dot(k_ref[:, at], suffix, 1, 0)).astype(BF16)

        for one in store(m):
            one.start()

    steps = []
    for m in range(M):
        arrives = 23.0 * (m + 1) / M
        after = ((stage_c, 0), (stage_d, 1.2), (stage_e, 4.2), (stage_z, 9.5), (stage_f, 13), (stage_g, 14))
        steps += [(arrives + t, m, stage) for stage, t in after]
        steps.append((arrives + 23, m, stage_h))
        steps.append((2.0 + 2.5 * m, m, inside))
    pl.semaphore_wait(barrier, len(partners))
    for m in range(M):
        states(m)
    for _, m, stage in sorted(steps, key=lambda step: step[:2]):
        stage(m)
    for m in range(M):
        for one in store(m):
            one.wait()
        for d in range(1, NY):
            y_in(m, d).wait_send()
            y_out_copy(m, d).wait_send()
        for d in range(1, NX):
            x_in_copy(m, d).wait_send()
            x_out_copy(m, d).wait_send()
        for d in range(1, NZ):
            z_copy(m, d).wait_send()
        core_in(m).wait_send()
        core_out_copy(m).wait_send()


def shards(queries, keys, values, grad_out):
    tokens = queries.shape[0]
    whole = pl.BlockSpec(memory_space=pl.ANY)
    dma = pltpu.SemaphoreType.DMA
    return pl.pallas_call(
        kernel,
        out_shape=[jax.ShapeDtypeStruct((tokens, H * DH), BF16)] * 3,
        in_specs=[whole] * 4,
        out_specs=[whole] * 3,
        scratch_shapes=[pltpu.VMEM((tokens, H * DH), BF16)] * 7
        + [
            pltpu.VMEM((M, NY, 2, R, DH), BF16),
            pltpu.VMEM((M, NY, 2, R, DH), BF16),
            pltpu.VMEM((M, R, DH), F32),
            pltpu.VMEM((M, R, DH), F32),
            pltpu.VMEM((M, R, DH), F32),
            pltpu.VMEM((M, NX, RX, DH), F32),
            pltpu.VMEM((M, NX, RX, DH), F32),
            pltpu.VMEM((M, NZ, RX, DH), BF16),
            pltpu.VMEM((M, NX, RX, DH), F32),
            pltpu.VMEM((M, NX, RX, DH), F32),
            pltpu.VMEM((M, R, DH), F32),
            pltpu.VMEM((M, R, DH), F32),
            pltpu.VMEM((M, NY, 2, R, DH), BF16),
            pltpu.VMEM((M, NY, 2, R, DH), BF16),
            pltpu.VMEM((tokens, H * DH), F32),
            pltpu.VMEM((tokens, H * DH), F32),
            pltpu.VMEM((tokens, H * DH), F32),
            dma((M, 4)), dma((M, 3)),
            dma((M, NY)), dma((M, NY)),
            dma((M,)), dma((M,)),
            dma((M, NX)), dma((M, NX)),
            dma((M, NZ)), dma((M, NZ)),
            dma((M, NX)), dma((M, NX)),
            dma((M,)), dma((M,)),
            dma((M, NY)), dma((M, NY)),
        ],
        compiler_params=pltpu.CompilerParams(
            collective_id=0, has_side_effects=True, vmem_limit_bytes=48 * 2**20
        ),
        cost_estimate=pl.CostEstimate(
            flops=20 * DH**3 * H, bytes_accessed=14 * tokens * H * DH, transcendentals=0
        ),
        name="scan",
    )(queries, keys, values, grad_out)


def solution(mesh):
    spec = P(("seq", "head"), None)
    return jax.shard_map(
        shards, mesh=mesh, in_specs=(spec,) * 4, out_specs=(spec,) * 3, check_vma=False
    )
```

```python
import jax
import jax.numpy as jnp
from jax import lax
from jax.experimental import pallas as pl
from jax.experimental.pallas import tpu as pltpu
from jax.sharding import PartitionSpec as P

H = 32
DH = 128
NZ, NX, NY = 8, 4, 4
PER = H // NY
M = 4
HC = PER // M
WIDE = NY * HC * DH
R = HC * DH
RX = R // NX
UNROLL = 4
MESH = pl.DeviceIdType.MESH
F32 = jnp.float32
BF16 = jnp.bfloat16


def dot(left, right, left_dim, right_dim):
    return lax.dot_general(
        left, right, (((left_dim,), (right_dim,)), ((), ())), preferred_element_type=F32
    )


def kernel(
    q_hbm, k_hbm, v_hbm, g_hbm, oq_hbm, ok_hbm, ov_hbm,
    q_ref, k_ref, v_ref, g_ref, oq_ref, ok_ref, ov_ref, sent, got, own_total, other_total, core_out, x_out, x_in, z_buf, x_back, base, base_out, base_other,
    y_out, final, part_q, part_k, part_v,
    in_sem, out_sem, yi_s, yi_r, c1_s, c1_r, xi_s, xi_r, zz_s, zz_r, xo_s, xo_r, c2_s, c2_r, yo_s, yo_r,
):
    s = lax.axis_index("seq")
    y = lax.axis_index("head")
    c = lax.rem(s, 2)
    x = lax.rem(s // 2, NX)
    z = s // (2 * NX)
    forward = c == 0
    mate = (s + 1 - 2 * c, y)

    def at_y(d):
        return lax.rem(y + d, NY)

    def at_x(d):
        return lax.rem(x + d, NX)

    def at_z(d):
        return lax.rem(z + d, NZ)

    def x_dev(i):
        return ((z * NX + i) * 2 + c, y)

    def z_dev(i):
        return ((i * NX + x) * 2 + c, y)

    def copy(src, dst, send, recv, device):
        return pltpu.make_async_remote_copy(
            src_ref=src, dst_ref=dst, send_sem=send, recv_sem=recv, device_id=device, device_id_type=MESH
        )

    barrier = pltpu.get_barrier_semaphore()
    partners = (
        [mate]
        + [(s, at_y(d)) for d in range(1, NY)]
        + [x_dev(at_x(d)) for d in range(1, NX)]
        + [z_dev(at_z(d)) for d in range(1, NZ)]
    )
    for partner in partners:
        pl.semaphore_signal(barrier, inc=1, device_id=partner, device_id_type=MESH)

    def lanes(m, owner, i):
        return pl.ds(pl.multiple_of(((m * NY + owner) * HC + i) * DH, DH), DH)

    def load(m):
        columns = slice(m * WIDE, (m + 1) * WIDE)
        pairs = ((k_hbm, k_ref), (v_hbm, v_ref), (q_hbm, q_ref), (g_hbm, g_ref))
        return [
            pltpu.make_async_copy(a.at[:, columns], b.at[:, columns], in_sem.at[m, n])
            for n, (a, b) in enumerate(pairs)
        ]

    def store(m):
        columns = slice(m * WIDE, (m + 1) * WIDE)
        pairs = ((oq_ref, oq_hbm), (ok_ref, ok_hbm), (ov_ref, ov_hbm))
        return [
            pltpu.make_async_copy(a.at[:, columns], b.at[:, columns], out_sem.at[m, n])
            for n, (a, b) in enumerate(pairs)
        ]

    for m in range(M):
        for one in load(m):
            one.start()

    def y_in(m, d, receive=False):
        slot = at_y(NY - d) if receive else y
        return copy(sent.at[m, at_y(d)], got.at[m, slot], yi_s.at[m, d], yi_r.at[m, d], (s, at_y(d)))

    def core_in(m):
        return copy(core_out.at[m], other_total.at[m], c1_s.at[m], c1_r.at[m], mate)

    def x_in_copy(m, d, receive=False):
        slot = at_x(NX - d) if receive else x
        return copy(x_out.at[m, at_x(d)], x_in.at[m, slot], xi_s.at[m, d], xi_r.at[m, d], x_dev(at_x(d)))

    def z_copy(m, d, receive=False):
        slot = at_z(NZ - d) if receive else z
        return copy(z_buf.at[m, z], z_buf.at[m, slot], zz_s.at[m, d], zz_r.at[m, d], z_dev(at_z(d)))

    def x_out_copy(m, d, receive=False):
        slot = at_x(NX - d) if receive else x
        return copy(x_back.at[m, at_x(d)], base.at[m, slot], xo_s.at[m, d], xo_r.at[m, d], x_dev(at_x(d)))

    def core_out_copy(m):
        return copy(base_out.at[m], base_other.at[m], c2_s.at[m], c2_r.at[m], mate)

    def y_out_copy(m, d, receive=False):
        slot = at_y(NY - d) if receive else y
        return copy(y_out.at[m, at_y(d)], final.at[m, slot], yo_s.at[m, d], yo_r.at[m, d], (s, at_y(d)))

    def states(m):
        for one in load(m):
            one.wait()
        for d in (2, 1, 3, 0):
            owner = at_y(d)
            for i in range(HC):
                at = lanes(m, owner, i)
                rows = slice(i * DH, (i + 1) * DH)
                key_state = dot(k_ref[:, at], v_ref[:, at], 0, 0).astype(BF16)
                grad_state = dot(q_ref[:, at], g_ref[:, at], 0, 0).astype(BF16)
                if d:
                    sent[m, owner, 0, rows, :] = key_state
                    sent[m, owner, 1, rows, :] = grad_state
                else:
                    got[m, y, 0, rows, :] = key_state
                    got[m, y, 1, rows, :] = grad_state
            if d:
                y_in(m, d).start()

    def inside(m):
        row = lax.broadcasted_iota(jnp.int32, (DH, DH), 0)
        column = lax.broadcasted_iota(jnp.int32, (DH, DH), 1)
        causal = column <= row

        @pl.loop(0, NY * HC // UNROLL)
        def _(n):
            for u in range(UNROLL):
                at = lanes(m, 0, n * UNROLL + u)
                q, k, v, g = q_ref[:, at], k_ref[:, at], v_ref[:, at], g_ref[:, at]
                grad_scores = jnp.where(causal, dot(g, v, 1, 1), 0.0).astype(BF16)
                query_scores = jnp.where(causal, dot(q, k, 1, 1), 0.0).astype(BF16)
                part_q[:, at] = dot(grad_scores, k, 1, 0)
                part_k[:, at] = dot(grad_scores, q, 0, 0)
                part_v[:, at] = dot(query_scores, g, 0, 0)

    def stage_c(m):
        for d in range(1, NY):
            y_in(m, d, True).wait_recv()

        @pl.loop(0, HC)
        def _(i):
            rows = pl.ds(pl.multiple_of(i * DH, DH), DH)
            totals = []
            for kind in range(2):
                total = got[m, 0, kind, rows, :].astype(F32)
                for j in range(1, NY):
                    total += got[m, j, kind, rows, :].astype(F32)
                totals.append(total)
            own_total[m, rows, :] = jnp.where(forward, totals[0], totals[1])
            core_out[m, rows, :] = jnp.where(forward, totals[1], totals[0])

        core_in(m).start()

    def stage_d(m):
        core_in(m).wait_recv()
        for i in range(NX):
            rows = slice(i * RX, (i + 1) * RX)
            x_out[m, i] = own_total[m, rows, :] + other_total[m, rows, :]
        for d in range(1, NX):
            x_in_copy(m, d).start()
        x_in[m, x] = x_out[m, x]

    def stage_e(m):
        for d in range(1, NX):
            x_in_copy(m, d, True).wait_recv()
        total = x_in[m, 0]
        for i in range(1, NX):
            total += x_in[m, i]
        z_buf[m, z] = total.astype(BF16)
        for d in range(1, NZ):
            z_copy(m, d).start()

    def stage_z(m):
        for d in range(1, NZ):
            z_copy(m, d, True).wait_recv()
        before = jnp.zeros((RX, DH), F32)
        for i in range(NZ):
            wanted = jnp.where(forward, i < z, i > z)
            before += jnp.where(wanted, z_buf[m, i].astype(F32), 0.0)
        ahead = [before]
        behind = [before]
        for i in range(NX - 1):
            ahead.append(ahead[-1] + x_in[m, i])
            behind.append(behind[-1] + x_in[m, NX - 1 - i])
        for i in range(NX):
            x_back[m, i] = jnp.where(forward, ahead[i], behind[NX - 1 - i])
        for d in range(1, NX):
            x_out_copy(m, d).start()
        base[m, x] = x_back[m, x]

    def stage_f(m):
        for d in range(1, NX):
            x_out_copy(m, d, True).wait_recv()
        for i in range(NX):
            rows = slice(i * RX, (i + 1) * RX)
            base_out[m, rows, :] = base[m, i] + own_total[m, rows, :]
        core_out_copy(m).start()

    def stage_g(m):
        core_out_copy(m).wait_recv()
        for i in range(NX):
            rows = slice(i * RX, (i + 1) * RX)
            mine = base[m, i]
            theirs = base_other[m, rows, :]
            run = jnp.where(forward, mine, theirs)
            for j in range(NY):
                y_out[m, j, 0, rows, :] = run.astype(BF16)
                if j < NY - 1:
                    run += got[m, j, 0, rows, :].astype(F32)
            run = jnp.where(forward, theirs, mine)
            for j in range(NY - 1, -1, -1):
                y_out[m, j, 1, rows, :] = run.astype(BF16)
                if j:
                    run += got[m, j, 1, rows, :].astype(F32)
        for d in (2, 1, 3):
            y_out_copy(m, d).start()
        final[m, y] = y_out[m, y]

    def stage_h(m):
        for d in range(1, NY):
            y_out_copy(m, d, True).wait_recv()

        @pl.loop(0, NY * HC // UNROLL)
        def _(n):
            for u in range(UNROLL):
                owner, i = (n * UNROLL + u) // HC, lax.rem(n * UNROLL + u, HC)
                at = lanes(m, owner, i)
                rows = pl.ds(pl.multiple_of(i * DH, DH), DH)
                prefix = final[m, owner, 0, rows, :]
                suffix = final[m, owner, 1, rows, :]
                oq_ref[:, at] = (part_q[:, at] + dot(g_ref[:, at], prefix, 1, 1)).astype(BF16)
                ok_ref[:, at] = (part_k[:, at] + dot(v_ref[:, at], suffix, 1, 1)).astype(BF16)
                ov_ref[:, at] = (part_v[:, at] + dot(k_ref[:, at], suffix, 1, 0)).astype(BF16)

        for one in store(m):
            one.start()

    steps = []
    for m in range(M):
        arrives = 23.0 * (m + 1) / M
        after = ((stage_c, 0), (stage_d, 1.2), (stage_e, 4.2), (stage_z, 9.5), (stage_f, 13), (stage_g, 14))
        steps += [(arrives + t, m, stage) for stage, t in after]
        steps.append((arrives + 23, m, stage_h))
        steps.append((2.0 + 2.5 * m, m, inside))
    pl.semaphore_wait(barrier, len(partners))
    for m in range(M):
        states(m)
    for _, m, stage in sorted(steps, key=lambda step: step[:2]):
        stage(m)
    for m in range(M):
        for one in store(m):
            one.wait()
        for d in range(1, NY):
            y_in(m, d).wait_send()
            y_out_copy(m, d).wait_send()
        for d in range(1, NX):
            x_in_copy(m, d).wait_send()
            x_out_copy(m, d).wait_send()
        for d in range(1, NZ):
            z_copy(m, d).wait_send()
        core_in(m).wait_send()
        core_out_copy(m).wait_send()


def shards(queries, keys, values, grad_out):
    tokens = queries.shape[0]
    whole = pl.BlockSpec(memory_space=pl.ANY)
    dma = pltpu.SemaphoreType.DMA
    return pl.pallas_call(
        kernel,
        out_shape=[jax.ShapeDtypeStruct((tokens, H * DH), BF16)] * 3,
        in_specs=[whole] * 4,
        out_specs=[whole] * 3,
        scratch_shapes=[pltpu.VMEM((tokens, H * DH), BF16)] * 7
        + [
            pltpu.VMEM((M, NY, 2, R, DH), BF16),
            pltpu.VMEM((M, NY, 2, R, DH), BF16),
            pltpu.VMEM((M, R, DH), F32),
            pltpu.VMEM((M, R, DH), F32),
            pltpu.VMEM((M, R, DH), F32),
            pltpu.VMEM((M, NX, RX, DH), F32),
            pltpu.VMEM((M, NX, RX, DH), F32),
            pltpu.VMEM((M, NZ, RX, DH), BF16),
            pltpu.VMEM((M, NX, RX, DH), F32),
            pltpu.VMEM((M, NX, RX, DH), F32),
            pltpu.VMEM((M, R, DH), F32),
            pltpu.VMEM((M, R, DH), F32),
            pltpu.VMEM((M, NY, 2, R, DH), BF16),
            pltpu.VMEM((M, NY, 2, R, DH), BF16),
            pltpu.VMEM((tokens, H * DH), F32),
            pltpu.VMEM((tokens, H * DH), F32),
            pltpu.VMEM((tokens, H * DH), F32),
            dma((M, 4)), dma((M, 3)),
            dma((M, NY)), dma((M, NY)),
            dma((M,)), dma((M,)),
            dma((M, NX)), dma((M, NX)),
            dma((M, NZ)), dma((M, NZ)),
            dma((M, NX)), dma((M, NX)),
            dma((M,)), dma((M,)),
            dma((M, NY)), dma((M, NY)),
        ],
        compiler_params=pltpu.CompilerParams(
            collective_id=0, has_side_effects=True, vmem_limit_bytes=63 * 2**20
        ),
        cost_estimate=pl.CostEstimate(
            flops=20 * DH**3 * H, bytes_accessed=14 * tokens * H * DH, transcendentals=0
        ),
        name="scan",
    )(queries, keys, values, grad_out)


def solution(mesh):
    spec = P(("seq", "head"), None)
    return jax.shard_map(
        shards, mesh=mesh, in_specs=(spec,) * 4, out_specs=(spec,) * 3, check_vma=False
    )
```

```python
import jax
import jax.numpy as jnp
from jax import lax
from jax.experimental import pallas as pl
from jax.experimental.pallas import tpu as pltpu
from jax.sharding import PartitionSpec as P

H = 32
DH = 128
NZ, NX, NY = 8, 4, 4
PER = H // NY
M = 4
HC = PER // M
WIDE = NY * HC * DH
R = HC * DH
RX = R // NX
UNROLL = 4
VMEM_MIB = 50
SPREAD = 1.0
Y_TIME = 23.0
MESH = pl.DeviceIdType.MESH
F32 = jnp.float32
BF16 = jnp.bfloat16


def dot(left, right, left_dim, right_dim):
    return lax.dot_general(
        left, right, (((left_dim,), (right_dim,)), ((), ())), preferred_element_type=F32
    )


def kernel(
    q_hbm, k_hbm, v_hbm, g_hbm, oq_hbm, ok_hbm, ov_hbm,
    q_ref, k_ref, v_ref, g_ref, oq_ref, ok_ref, ov_ref, sent, got, own_total, other_total, core_out, x_out, x_in, z_buf, z_sum, x_back, base, base_out, base_other,
    y_out, final, part_q, part_k, part_v,
    in_sem, out_sem, yi_s, yi_r, c1_s, c1_r, xi_s, xi_r, zz_s, zz_r, xo_s, xo_r, c2_s, c2_r, yo_s, yo_r,
):
    s = lax.axis_index("seq")
    y = lax.axis_index("head")
    c = lax.rem(s, 2)
    x = lax.rem(s // 2, NX)
    z = s // (2 * NX)
    forward = c == 0
    mate = (s + 1 - 2 * c, y)
    rank = jnp.where(forward, z, NZ - 1 - z)

    def at_y(d):
        return lax.rem(y + d, NY)

    def at_x(d):
        return lax.rem(x + d, NX)

    def x_dev(i):
        return ((z * NX + i) * 2 + c, y)

    def z_dev(place):
        return ((jnp.where(forward, place, NZ - 1 - place) * NX + x) * 2 + c, y)

    def copy(src, dst, send, recv, device):
        return pltpu.make_async_remote_copy(
            src_ref=src, dst_ref=dst, send_sem=send, recv_sem=recv, device_id=device, device_id_type=MESH
        )

    barrier = pltpu.get_barrier_semaphore()
    partners = (
        [mate]
        + [(s, at_y(d)) for d in range(1, NY)]
        + [x_dev(at_x(d)) for d in range(1, NX)]
        + [z_dev(lax.rem(rank + d, NZ)) for d in range(1, NZ)]
    )
    for partner in partners:
        pl.semaphore_signal(barrier, inc=1, device_id=partner, device_id_type=MESH)

    def lanes(m, owner, i):
        return pl.ds(pl.multiple_of(((m * NY + owner) * HC + i) * DH, DH), DH)

    def load(m):
        columns = slice(m * WIDE, (m + 1) * WIDE)
        pairs = ((k_hbm, k_ref), (v_hbm, v_ref), (q_hbm, q_ref), (g_hbm, g_ref))
        return [
            pltpu.make_async_copy(a.at[:, columns], b.at[:, columns], in_sem.at[m, n])
            for n, (a, b) in enumerate(pairs)
        ]

    def store(m):
        columns = slice(m * WIDE, (m + 1) * WIDE)
        pairs = ((oq_ref, oq_hbm), (ok_ref, ok_hbm), (ov_ref, ov_hbm))
        return [
            pltpu.make_async_copy(a.at[:, columns], b.at[:, columns], out_sem.at[m, n])
            for n, (a, b) in enumerate(pairs)
        ]

    for m in range(M):
        for one in load(m):
            one.start()

    def y_in(m, d, receive=False):
        slot = at_y(NY - d) if receive else y
        return copy(sent.at[m, at_y(d)], got.at[m, slot], yi_s.at[m, d], yi_r.at[m, d], (s, at_y(d)))

    def core_in(m):
        return copy(core_out.at[m], other_total.at[m], c1_s.at[m], c1_r.at[m], mate)

    def x_in_copy(m, d, receive=False):
        slot = at_x(NX - d) if receive else x
        return copy(x_out.at[m, at_x(d)], x_in.at[m, slot], xi_s.at[m, d], xi_r.at[m, d], x_dev(at_x(d)))

    def z_copy(m, d, receive=False):
        slot = rank - d if receive else rank
        device = z_dev(lax.rem(rank + d, NZ))
        return copy(z_buf.at[m, rank], z_buf.at[m, slot], zz_s.at[m, d], zz_r.at[m, d], device)

    def x_out_copy(m, d, receive=False):
        slot = at_x(NX - d) if receive else x
        return copy(x_back.at[m, at_x(d)], base.at[m, slot], xo_s.at[m, d], xo_r.at[m, d], x_dev(at_x(d)))

    def core_out_copy(m):
        return copy(base_out.at[m], base_other.at[m], c2_s.at[m], c2_r.at[m], mate)

    def y_out_copy(m, d, receive=False):
        slot = at_y(NY - d) if receive else y
        return copy(y_out.at[m, at_y(d)], final.at[m, slot], yo_s.at[m, d], yo_r.at[m, d], (s, at_y(d)))

    def states(m):
        for one in load(m):
            one.wait()
        for d in (2, 1, 3, 0):
            owner = at_y(d)
            for i in range(HC):
                at = lanes(m, owner, i)
                rows = slice(i * DH, (i + 1) * DH)
                key_state = dot(k_ref[:, at], v_ref[:, at], 0, 0).astype(BF16)
                grad_state = dot(q_ref[:, at], g_ref[:, at], 0, 0).astype(BF16)
                if d:
                    sent[m, owner, 0, rows, :] = key_state
                    sent[m, owner, 1, rows, :] = grad_state
                else:
                    got[m, y, 0, rows, :] = key_state
                    got[m, y, 1, rows, :] = grad_state
            if d:
                y_in(m, d).start()

    def inside(m):
        row = lax.broadcasted_iota(jnp.int32, (DH, DH), 0)
        column = lax.broadcasted_iota(jnp.int32, (DH, DH), 1)
        causal = column <= row

        @pl.loop(0, NY * HC // UNROLL)
        def _(n):
            for u in range(UNROLL):
                at = lanes(m, 0, n * UNROLL + u)
                q, k, v, g = q_ref[:, at], k_ref[:, at], v_ref[:, at], g_ref[:, at]
                grad_scores = jnp.where(causal, dot(g, v, 1, 1), 0.0).astype(BF16)
                query_scores = jnp.where(causal, dot(q, k, 1, 1), 0.0).astype(BF16)
                part_q[:, at] = dot(grad_scores, k, 1, 0)
                part_k[:, at] = dot(grad_scores, q, 0, 0)
                part_v[:, at] = dot(query_scores, g, 0, 0)

    def stage_c(m):
        for d in range(1, NY):
            y_in(m, d, True).wait_recv()

        @pl.loop(0, HC)
        def _(i):
            rows = pl.ds(pl.multiple_of(i * DH, DH), DH)
            totals = []
            for kind in range(2):
                total = got[m, 0, kind, rows, :].astype(F32)
                for j in range(1, NY):
                    total += got[m, j, kind, rows, :].astype(F32)
                totals.append(total)
            own_total[m, rows, :] = jnp.where(forward, totals[0], totals[1])
            core_out[m, rows, :] = jnp.where(forward, totals[1], totals[0])

        core_in(m).start()

    def stage_d(m):
        core_in(m).wait_recv()
        for i in range(NX):
            rows = slice(i * RX, (i + 1) * RX)
            x_out[m, i] = own_total[m, rows, :] + other_total[m, rows, :]
        for d in range(1, NX):
            x_in_copy(m, d).start()
        x_in[m, x] = x_out[m, x]

    def stage_e(m):
        for d in range(1, NX):
            x_in_copy(m, d, True).wait_recv()
        total = x_in[m, 0]
        for i in range(1, NX):
            total += x_in[m, i]
        z_buf[m, rank] = total.astype(BF16)
        for d in range(1, NZ):

            @pl.when(rank + d < NZ)
            def _():
                z_copy(m, d).start()

    def stage_z(m):
        z_sum[m] = jnp.zeros((RX, DH), F32)
        for d in range(1, NZ):

            @pl.when(rank - d >= 0)
            def _():
                z_copy(m, d, True).wait_recv()
                z_sum[m] += z_buf[m, rank - d].astype(F32)

        before = z_sum[m]
        ahead = [before]
        behind = [before]
        for i in range(NX - 1):
            ahead.append(ahead[-1] + x_in[m, i])
            behind.append(behind[-1] + x_in[m, NX - 1 - i])
        for i in range(NX):
            x_back[m, i] = jnp.where(forward, ahead[i], behind[NX - 1 - i])
        for d in range(1, NX):
            x_out_copy(m, d).start()
        base[m, x] = x_back[m, x]

    def stage_f(m):
        for d in range(1, NX):
            x_out_copy(m, d, True).wait_recv()
        for i in range(NX):
            rows = slice(i * RX, (i + 1) * RX)
            base_out[m, rows, :] = base[m, i] + own_total[m, rows, :]
        core_out_copy(m).start()

    def stage_g(m):
        core_out_copy(m).wait_recv()
        for i in range(NX):
            rows = slice(i * RX, (i + 1) * RX)
            mine = base[m, i]
            theirs = base_other[m, rows, :]
            run = jnp.where(forward, mine, theirs)
            for j in range(NY):
                y_out[m, j, 0, rows, :] = run.astype(BF16)
                if j < NY - 1:
                    run += got[m, j, 0, rows, :].astype(F32)
            run = jnp.where(forward, theirs, mine)
            for j in range(NY - 1, -1, -1):
                y_out[m, j, 1, rows, :] = run.astype(BF16)
                if j:
                    run += got[m, j, 1, rows, :].astype(F32)
        for d in (2, 1, 3):
            y_out_copy(m, d).start()
        final[m, y] = y_out[m, y]

    def stage_h(m):
        for d in range(1, NY):
            y_out_copy(m, d, True).wait_recv()

        @pl.loop(0, NY * HC // UNROLL)
        def _(n):
            for u in range(UNROLL):
                owner, i = (n * UNROLL + u) // HC, lax.rem(n * UNROLL + u, HC)
                at = lanes(m, owner, i)
                rows = pl.ds(pl.multiple_of(i * DH, DH), DH)
                prefix = final[m, owner, 0, rows, :]
                suffix = final[m, owner, 1, rows, :]
                oq_ref[:, at] = (part_q[:, at] + dot(g_ref[:, at], prefix, 1, 1)).astype(BF16)
                ok_ref[:, at] = (part_k[:, at] + dot(v_ref[:, at], suffix, 1, 1)).astype(BF16)
                ov_ref[:, at] = (part_v[:, at] + dot(k_ref[:, at], suffix, 1, 0)).astype(BF16)

        for one in store(m):
            one.start()

    steps = []
    for m in range(M):
        arrives = Y_TIME * (m + 1) / M
        after = ((stage_c, 0), (stage_d, 1.2), (stage_e, 4.2), (stage_z, 9.5), (stage_f, 13), (stage_g, 14))
        steps += [(arrives + SPREAD * t, m, stage) for stage, t in after]
        steps.append((arrives + 23, m, stage_h))
        steps.append((2.0 + 2.5 * m, m, inside))
    pl.semaphore_wait(barrier, len(partners))
    for m in range(M):
        states(m)
    for _, m, stage in sorted(steps, key=lambda step: step[:2]):
        stage(m)
    for m in range(M):
        for one in store(m):
            one.wait()
        for d in range(1, NY):
            y_in(m, d).wait_send()
            y_out_copy(m, d).wait_send()
        for d in range(1, NX):
            x_in_copy(m, d).wait_send()
            x_out_copy(m, d).wait_send()
        for d in range(1, NZ):

            @pl.when(rank + d < NZ)
            def _():
                z_copy(m, d).wait_send()

        core_in(m).wait_send()
        core_out_copy(m).wait_send()


def finish(*refs):
    sources, targets, sem = refs[:3], refs[3:6], refs[6]
    copies = [pltpu.make_async_copy(a, b, sem.at[n]) for n, (a, b) in enumerate(zip(sources, targets))]
    for one in copies:
        one.start()
    for one in copies:
        one.wait()


def shards(queries, keys, values, grad_out):
    tokens = queries.shape[0]
    whole = pl.BlockSpec(memory_space=pl.ANY)
    dma = pltpu.SemaphoreType.DMA
    shapes = [jax.ShapeDtypeStruct((tokens, H * DH), BF16)] * 3
    results = pl.pallas_call(
        kernel,
        out_shape=shapes,
        in_specs=[whole] * 4,
        out_specs=[whole] * 3,
        scratch_shapes=[pltpu.VMEM((tokens, H * DH), BF16)] * 7
        + [
            pltpu.VMEM((M, NY, 2, R, DH), BF16),
            pltpu.VMEM((M, NY, 2, R, DH), BF16),
            pltpu.VMEM((M, R, DH), F32),
            pltpu.VMEM((M, R, DH), F32),
            pltpu.VMEM((M, R, DH), F32),
            pltpu.VMEM((M, NX, RX, DH), F32),
            pltpu.VMEM((M, NX, RX, DH), F32),
            pltpu.VMEM((M, NZ, RX, DH), BF16),
            pltpu.VMEM((M, RX, DH), F32),
            pltpu.VMEM((M, NX, RX, DH), F32),
            pltpu.VMEM((M, NX, RX, DH), F32),
            pltpu.VMEM((M, R, DH), F32),
            pltpu.VMEM((M, R, DH), F32),
            pltpu.VMEM((M, NY, 2, R, DH), BF16),
            pltpu.VMEM((M, NY, 2, R, DH), BF16),
            pltpu.VMEM((tokens, H * DH), F32),
            pltpu.VMEM((tokens, H * DH), F32),
            pltpu.VMEM((tokens, H * DH), F32),
            dma((M, 4)), dma((M, 3)),
            dma((M, NY)), dma((M, NY)),
            dma((M,)), dma((M,)),
            dma((M, NX)), dma((M, NX)),
            dma((M, NZ)), dma((M, NZ)),
            dma((M, NX)), dma((M, NX)),
            dma((M,)), dma((M,)),
            dma((M, NY)), dma((M, NY)),
        ],
        compiler_params=pltpu.CompilerParams(
            collective_id=0, has_side_effects=True, vmem_limit_bytes=VMEM_MIB * 2**20
        ),
        cost_estimate=pl.CostEstimate(
            flops=20 * DH**3 * H, bytes_accessed=14 * tokens * H * DH, transcendentals=0
        ),
        name="scan",
    )(queries, keys, values, grad_out)
    return pl.pallas_call(
        finish,
        out_shape=shapes,
        in_specs=[whole] * 3,
        out_specs=[whole] * 3,
        scratch_shapes=[dma((3,))],
        cost_estimate=pl.CostEstimate(flops=0, bytes_accessed=12 * tokens * H * DH, transcendentals=0),
        name="finish",
    )(*results)


def solution(mesh):
    spec = P(("seq", "head"), None)
    return jax.shard_map(
        shards, mesh=mesh, in_specs=(spec,) * 4, out_specs=(spec,) * 3, check_vma=False
    )
```

```python
import jax
import jax.numpy as jnp
from jax import lax
from jax.experimental import pallas as pl
from jax.experimental.pallas import tpu as pltpu
from jax.sharding import PartitionSpec as P

H = 32
DH = 128
NZ, NX, NY = 8, 4, 4
PER = H // NY
M = 4
HC = PER // M
WIDE = NY * HC * DH
R = HC * DH
RX = R // NX
UNROLL = 4
VMEM_MIB = 50
SPREAD = 1.0
Y_TIME = 23.0
MESH = pl.DeviceIdType.MESH
F32 = jnp.float32
BF16 = jnp.bfloat16


def dot(left, right, left_dim, right_dim):
    return lax.dot_general(
        left, right, (((left_dim,), (right_dim,)), ((), ())), preferred_element_type=F32
    )


def kernel(
    q_hbm, k_hbm, v_hbm, g_hbm, oq_hbm, ok_hbm, ov_hbm,
    q_ref, k_ref, v_ref, g_ref, oq_ref, ok_ref, ov_ref, sent, got, own_total, other_total, core_out, x_out, x_in, z_buf, z_sum, x_back, base, base_out, base_other,
    y_out, final, part_q, part_k, part_v,
    in_sem, out_sem, yi_s, yi_r, c1_s, c1_r, xi_s, xi_r, zz_s, zz_r, xo_s, xo_r, c2_s, c2_r, yo_s, yo_r,
):
    s = lax.axis_index("seq")
    y = lax.axis_index("head")
    c = lax.rem(s, 2)
    x = lax.rem(s // 2, NX)
    z = s // (2 * NX)
    forward = c == 0
    mate = (s + 1 - 2 * c, y)
    rank = jnp.where(forward, z, NZ - 1 - z)

    def at_y(d):
        return lax.rem(y + d, NY)

    def at_x(d):
        return lax.rem(x + d, NX)

    def x_dev(i):
        return ((z * NX + i) * 2 + c, y)

    def z_dev(place):
        return ((jnp.where(forward, place, NZ - 1 - place) * NX + x) * 2 + c, y)

    def copy(src, dst, send, recv, device):
        return pltpu.make_async_remote_copy(
            src_ref=src, dst_ref=dst, send_sem=send, recv_sem=recv, device_id=device, device_id_type=MESH
        )

    barrier = pltpu.get_barrier_semaphore()
    partners = (
        [mate]
        + [(s, at_y(d)) for d in range(1, NY)]
        + [x_dev(at_x(d)) for d in range(1, NX)]
        + [z_dev(lax.rem(rank + d, NZ)) for d in range(1, NZ)]
    )
    for partner in partners:
        pl.semaphore_signal(barrier, inc=1, device_id=partner, device_id_type=MESH)

    def lanes(m, owner, i):
        return pl.ds(pl.multiple_of(((m * NY + owner) * HC + i) * DH, DH), DH)

    def load(m):
        columns = slice(m * WIDE, (m + 1) * WIDE)
        pairs = ((k_hbm, k_ref), (v_hbm, v_ref), (q_hbm, q_ref), (g_hbm, g_ref))
        return [
            pltpu.make_async_copy(a.at[:, columns], b.at[:, columns], in_sem.at[m, n])
            for n, (a, b) in enumerate(pairs)
        ]

    def store(m):
        columns = slice(m * WIDE, (m + 1) * WIDE)
        pairs = ((oq_ref, oq_hbm), (ok_ref, ok_hbm), (ov_ref, ov_hbm))
        return [
            pltpu.make_async_copy(a.at[:, columns], b.at[:, columns], out_sem.at[m, n])
            for n, (a, b) in enumerate(pairs)
        ]

    for m in range(M):
        for one in load(m):
            one.start()

    def y_in(m, d, receive=False):
        slot = at_y(NY - d) if receive else y
        return copy(sent.at[m, at_y(d)], got.at[m, slot], yi_s.at[m, d], yi_r.at[m, d], (s, at_y(d)))

    def core_in(m):
        return copy(core_out.at[m], other_total.at[m], c1_s.at[m], c1_r.at[m], mate)

    def x_in_copy(m, d, receive=False):
        slot = at_x(NX - d) if receive else x
        return copy(x_out.at[m, at_x(d)], x_in.at[m, slot], xi_s.at[m, d], xi_r.at[m, d], x_dev(at_x(d)))

    def z_copy(m, d, receive=False):
        slot = rank - d if receive else rank
        device = z_dev(lax.rem(rank + d, NZ))
        return copy(z_buf.at[m, rank], z_buf.at[m, slot], zz_s.at[m, d], zz_r.at[m, d], device)

    def x_out_copy(m, d, receive=False):
        slot = at_x(NX - d) if receive else x
        return copy(x_back.at[m, at_x(d)], base.at[m, slot], xo_s.at[m, d], xo_r.at[m, d], x_dev(at_x(d)))

    def core_out_copy(m):
        return copy(base_out.at[m], base_other.at[m], c2_s.at[m], c2_r.at[m], mate)

    def y_out_copy(m, d, receive=False):
        slot = at_y(NY - d) if receive else y
        return copy(y_out.at[m, at_y(d)], final.at[m, slot], yo_s.at[m, d], yo_r.at[m, d], (s, at_y(d)))

    def states(m):
        for one in load(m):
            one.wait()
        for d in (2, 1, 3, 0):
            owner = at_y(d)
            for i in range(HC):
                at = lanes(m, owner, i)
                rows = slice(i * DH, (i + 1) * DH)
                key_state = dot(k_ref[:, at], v_ref[:, at], 0, 0).astype(BF16)
                grad_state = dot(q_ref[:, at], g_ref[:, at], 0, 0).astype(BF16)
                if d:
                    sent[m, owner, 0, rows, :] = key_state
                    sent[m, owner, 1, rows, :] = grad_state
                else:
                    got[m, y, 0, rows, :] = key_state
                    got[m, y, 1, rows, :] = grad_state
            if d:
                y_in(m, d).start()

    def inside(m):
        row = lax.broadcasted_iota(jnp.int32, (DH, DH), 0)
        column = lax.broadcasted_iota(jnp.int32, (DH, DH), 1)
        causal = column <= row

        @pl.loop(0, NY * HC // UNROLL)
        def _(n):
            for u in range(UNROLL):
                at = lanes(m, 0, n * UNROLL + u)
                q, k, v, g = q_ref[:, at], k_ref[:, at], v_ref[:, at], g_ref[:, at]
                grad_scores = jnp.where(causal, dot(g, v, 1, 1), 0.0).astype(BF16)
                query_scores = jnp.where(causal, dot(q, k, 1, 1), 0.0).astype(BF16)
                part_q[:, at] = dot(grad_scores, k, 1, 0)
                part_k[:, at] = dot(grad_scores, q, 0, 0)
                part_v[:, at] = dot(query_scores, g, 0, 0)

    def stage_c(m):
        for d in range(1, NY):
            y_in(m, d, True).wait_recv()

        @pl.loop(0, HC)
        def _(i):
            rows = pl.ds(pl.multiple_of(i * DH, DH), DH)
            totals = []
            for kind in range(2):
                total = got[m, 0, kind, rows, :].astype(F32)
                for j in range(1, NY):
                    total += got[m, j, kind, rows, :].astype(F32)
                totals.append(total)
            own_total[m, rows, :] = jnp.where(forward, totals[0], totals[1])
            core_out[m, rows, :] = jnp.where(forward, totals[1], totals[0])

        core_in(m).start()

    def stage_d(m):
        core_in(m).wait_recv()
        for i in range(NX):
            rows = slice(i * RX, (i + 1) * RX)
            x_out[m, i] = own_total[m, rows, :] + other_total[m, rows, :]
        for d in range(1, NX):
            x_in_copy(m, d).start()
        x_in[m, x] = x_out[m, x]

    def stage_e(m):
        for d in range(1, NX):
            x_in_copy(m, d, True).wait_recv()
        total = x_in[m, 0]
        for i in range(1, NX):
            total += x_in[m, i]
        z_buf[m, rank] = total.astype(BF16)
        for d in range(1, NZ):

            @pl.when(rank + d < NZ)
            def _():
                z_copy(m, d).start()

    def stage_z(m):
        z_sum[m] = jnp.zeros((RX, DH), F32)
        for d in range(1, NZ):

            @pl.when(rank - d >= 0)
            def _():
                z_copy(m, d, True).wait_recv()
                z_sum[m] += z_buf[m, rank - d].astype(F32)

        before = z_sum[m]
        ahead = [before]
        behind = [before]
        for i in range(NX - 1):
            ahead.append(ahead[-1] + x_in[m, i])
            behind.append(behind[-1] + x_in[m, NX - 1 - i])
        for i in range(NX):
            x_back[m, i] = jnp.where(forward, ahead[i], behind[NX - 1 - i])
        for d in range(1, NX):
            x_out_copy(m, d).start()
        base[m, x] = x_back[m, x]

    def stage_f(m):
        for d in range(1, NX):
            x_out_copy(m, d, True).wait_recv()
        for i in range(NX):
            rows = slice(i * RX, (i + 1) * RX)
            base_out[m, rows, :] = base[m, i] + own_total[m, rows, :]
        core_out_copy(m).start()

    def stage_g(m):
        core_out_copy(m).wait_recv()
        for i in range(NX):
            rows = slice(i * RX, (i + 1) * RX)
            mine = base[m, i]
            theirs = base_other[m, rows, :]
            run = jnp.where(forward, mine, theirs)
            for j in range(NY):
                y_out[m, j, 0, rows, :] = run.astype(BF16)
                if j < NY - 1:
                    run += got[m, j, 0, rows, :].astype(F32)
            run = jnp.where(forward, theirs, mine)
            for j in range(NY - 1, -1, -1):
                y_out[m, j, 1, rows, :] = run.astype(BF16)
                if j:
                    run += got[m, j, 1, rows, :].astype(F32)
        for d in (2, 1, 3):
            y_out_copy(m, d).start()
        final[m, y] = y_out[m, y]

    def stage_h(m):
        for d in range(1, NY):
            y_out_copy(m, d, True).wait_recv()

        @pl.loop(0, NY * HC // UNROLL)
        def _(n):
            for u in range(UNROLL):
                owner, i = (n * UNROLL + u) // HC, lax.rem(n * UNROLL + u, HC)
                at = lanes(m, owner, i)
                rows = pl.ds(pl.multiple_of(i * DH, DH), DH)
                prefix = final[m, owner, 0, rows, :]
                suffix = final[m, owner, 1, rows, :]
                oq_ref[:, at] = (part_q[:, at] + dot(g_ref[:, at], prefix, 1, 1)).astype(BF16)
                ok_ref[:, at] = (part_k[:, at] + dot(v_ref[:, at], suffix, 1, 1)).astype(BF16)
                ov_ref[:, at] = (part_v[:, at] + dot(k_ref[:, at], suffix, 1, 0)).astype(BF16)

        for one in store(m):
            one.start()

    steps = []
    for m in range(M):
        arrives = Y_TIME * (m + 1) / M
        after = ((stage_c, 0), (stage_d, 1.2), (stage_e, 4.2), (stage_z, 9.5), (stage_f, 13), (stage_g, 14))
        steps += [(arrives + SPREAD * t, m, stage) for stage, t in after]
        steps.append((arrives + 23, m, stage_h))
        steps.append((2.0 + 2.5 * m, m, inside))
    pl.semaphore_wait(barrier, len(partners))
    for m in range(M):
        states(m)
    for _, m, stage in sorted(steps, key=lambda step: step[:2]):
        stage(m)
    for m in range(M):
        for one in store(m):
            one.wait()
        for d in range(1, NY):
            y_in(m, d).wait_send()
            y_out_copy(m, d).wait_send()
        for d in range(1, NX):
            x_in_copy(m, d).wait_send()
            x_out_copy(m, d).wait_send()
        for d in range(1, NZ):

            @pl.when(rank + d < NZ)
            def _():
                z_copy(m, d).wait_send()

        core_in(m).wait_send()
        core_out_copy(m).wait_send()


def finish(*refs):
    sources, targets, sem = refs[:3], refs[3:6], refs[6]
    copies = [pltpu.make_async_copy(a, b, sem.at[n]) for n, (a, b) in enumerate(zip(sources, targets))]
    for one in copies:
        one.start()
    for one in copies:
        one.wait()


def shards(queries, keys, values, grad_out):
    tokens = queries.shape[0]
    whole = pl.BlockSpec(memory_space=pl.ANY)
    dma = pltpu.SemaphoreType.DMA
    shapes = [jax.ShapeDtypeStruct((tokens, H * DH), BF16)] * 3
    return pl.pallas_call(
        kernel,
        out_shape=shapes,
        in_specs=[whole] * 4,
        out_specs=[whole] * 3,
        scratch_shapes=[pltpu.VMEM((tokens, H * DH), BF16)] * 7
        + [
            pltpu.VMEM((M, NY, 2, R, DH), BF16),
            pltpu.VMEM((M, NY, 2, R, DH), BF16),
            pltpu.VMEM((M, R, DH), F32),
            pltpu.VMEM((M, R, DH), F32),
            pltpu.VMEM((M, R, DH), F32),
            pltpu.VMEM((M, NX, RX, DH), F32),
            pltpu.VMEM((M, NX, RX, DH), F32),
            pltpu.VMEM((M, NZ, RX, DH), BF16),
            pltpu.VMEM((M, RX, DH), F32),
            pltpu.VMEM((M, NX, RX, DH), F32),
            pltpu.VMEM((M, NX, RX, DH), F32),
            pltpu.VMEM((M, R, DH), F32),
            pltpu.VMEM((M, R, DH), F32),
            pltpu.VMEM((M, NY, 2, R, DH), BF16),
            pltpu.VMEM((M, NY, 2, R, DH), BF16),
            pltpu.VMEM((tokens, H * DH), F32),
            pltpu.VMEM((tokens, H * DH), F32),
            pltpu.VMEM((tokens, H * DH), F32),
            dma((M, 4)), dma((M, 3)),
            dma((M, NY)), dma((M, NY)),
            dma((M,)), dma((M,)),
            dma((M, NX)), dma((M, NX)),
            dma((M, NZ)), dma((M, NZ)),
            dma((M, NX)), dma((M, NX)),
            dma((M,)), dma((M,)),
            dma((M, NY)), dma((M, NY)),
        ],
        compiler_params=pltpu.CompilerParams(
            collective_id=0, has_side_effects=True, vmem_limit_bytes=VMEM_MIB * 2**20
        ),
        cost_estimate=pl.CostEstimate(
            flops=20 * DH**3 * H, bytes_accessed=14 * tokens * H * DH, transcendentals=0
        ),
        name="scan",
    )(queries, keys, values, grad_out)

def solution(mesh):
    spec = P(("seq", "head"), None)
    return jax.shard_map(
        shards, mesh=mesh, in_specs=(spec,) * 4, out_specs=(spec,) * 3, check_vma=False
    )
```

```python
import jax
import jax.numpy as jnp
from jax import lax
from jax.experimental import pallas as pl
from jax.experimental.pallas import tpu as pltpu
from jax.sharding import PartitionSpec as P

H = 32
DH = 128
NZ, NX, NY = 8, 4, 4
PER = H // NY
M = 4
HC = PER // M
WIDE = NY * HC * DH
R = HC * DH
RX = R // NX
UNROLL = 4
VMEM_MIB = 50
SPREAD = 1.0
Y_TIME = 23.0
MESH = pl.DeviceIdType.MESH
F32 = jnp.float32
BF16 = jnp.bfloat16


def dot(left, right, left_dim, right_dim):
    return lax.dot_general(
        left, right, (((left_dim,), (right_dim,)), ((), ())), preferred_element_type=F32
    )


def kernel(
    q_hbm, k_hbm, v_hbm, g_hbm, oq_ref, ok_ref, ov_ref,
    q_ref, k_ref, v_ref, g_ref, sent, got, own_total, other_total, core_out, x_out, x_in, z_buf, z_sum, x_back, base, base_out, base_other,
    y_out, final, part_q, part_k, part_v,
    in_sem, yi_s, yi_r, c1_s, c1_r, xi_s, xi_r, zz_s, zz_r, xo_s, xo_r, c2_s, c2_r, yo_s, yo_r,
):
    s = lax.axis_index("seq")
    y = lax.axis_index("head")
    c = lax.rem(s, 2)
    x = lax.rem(s // 2, NX)
    z = s // (2 * NX)
    forward = c == 0
    mate = (s + 1 - 2 * c, y)
    rank = jnp.where(forward, z, NZ - 1 - z)

    def at_y(d):
        return lax.rem(y + d, NY)

    def at_x(d):
        return lax.rem(x + d, NX)

    def x_dev(i):
        return ((z * NX + i) * 2 + c, y)

    def z_dev(place):
        return ((jnp.where(forward, place, NZ - 1 - place) * NX + x) * 2 + c, y)

    def copy(src, dst, send, recv, device):
        return pltpu.make_async_remote_copy(
            src_ref=src, dst_ref=dst, send_sem=send, recv_sem=recv, device_id=device, device_id_type=MESH
        )

    barrier = pltpu.get_barrier_semaphore()
    partners = (
        [mate]
        + [(s, at_y(d)) for d in range(1, NY)]
        + [x_dev(at_x(d)) for d in range(1, NX)]
        + [z_dev(lax.rem(rank + d, NZ)) for d in range(1, NZ)]
    )
    for partner in partners:
        pl.semaphore_signal(barrier, inc=1, device_id=partner, device_id_type=MESH)

    def lanes(m, owner, i):
        return pl.ds(pl.multiple_of(((m * NY + owner) * HC + i) * DH, DH), DH)

    def load(m):
        columns = slice(m * WIDE, (m + 1) * WIDE)
        pairs = ((k_hbm, k_ref), (v_hbm, v_ref), (q_hbm, q_ref), (g_hbm, g_ref))
        return [
            pltpu.make_async_copy(a.at[:, columns], b.at[:, columns], in_sem.at[m, n])
            for n, (a, b) in enumerate(pairs)
        ]

    for m in range(M):
        for one in load(m):
            one.start()

    def y_in(m, d, receive=False):
        slot = at_y(NY - d) if receive else y
        return copy(sent.at[m, at_y(d)], got.at[m, slot], yi_s.at[m, d], yi_r.at[m, d], (s, at_y(d)))

    def core_in(m):
        return copy(core_out.at[m], other_total.at[m], c1_s.at[m], c1_r.at[m], mate)

    def x_in_copy(m, d, receive=False):
        slot = at_x(NX - d) if receive else x
        return copy(x_out.at[m, at_x(d)], x_in.at[m, slot], xi_s.at[m, d], xi_r.at[m, d], x_dev(at_x(d)))

    def z_copy(m, d, receive=False):
        slot = rank - d if receive else rank
        device = z_dev(lax.rem(rank + d, NZ))
        return copy(z_buf.at[m, rank], z_buf.at[m, slot], zz_s.at[m, d], zz_r.at[m, d], device)

    def x_out_copy(m, d, receive=False):
        slot = at_x(NX - d) if receive else x
        return copy(x_back.at[m, at_x(d)], base.at[m, slot], xo_s.at[m, d], xo_r.at[m, d], x_dev(at_x(d)))

    def core_out_copy(m):
        return copy(base_out.at[m], base_other.at[m], c2_s.at[m], c2_r.at[m], mate)

    def y_out_copy(m, d, receive=False):
        slot = at_y(NY - d) if receive else y
        return copy(y_out.at[m, at_y(d)], final.at[m, slot], yo_s.at[m, d], yo_r.at[m, d], (s, at_y(d)))

    def states(m):
        for one in load(m):
            one.wait()
        for d in (2, 1, 3, 0):
            owner = at_y(d)
            for i in range(HC):
                at = lanes(m, owner, i)
                rows = slice(i * DH, (i + 1) * DH)
                key_state = dot(k_ref[:, at], v_ref[:, at], 0, 0).astype(BF16)
                grad_state = dot(q_ref[:, at], g_ref[:, at], 0, 0).astype(BF16)
                if d:
                    sent[m, owner, 0, rows, :] = key_state
                    sent[m, owner, 1, rows, :] = grad_state
                else:
                    got[m, y, 0, rows, :] = key_state
                    got[m, y, 1, rows, :] = grad_state
            if d:
                y_in(m, d).start()

    def inside(m):
        row = lax.broadcasted_iota(jnp.int32, (DH, DH), 0)
        column = lax.broadcasted_iota(jnp.int32, (DH, DH), 1)
        causal = column <= row

        @pl.loop(0, NY * HC // UNROLL)
        def _(n):
            for u in range(UNROLL):
                at = lanes(m, 0, n * UNROLL + u)
                q, k, v, g = q_ref[:, at], k_ref[:, at], v_ref[:, at], g_ref[:, at]
                grad_scores = jnp.where(causal, dot(g, v, 1, 1), 0.0).astype(BF16)
                query_scores = jnp.where(causal, dot(q, k, 1, 1), 0.0).astype(BF16)
                part_q[:, at] = dot(grad_scores, k, 1, 0)
                part_k[:, at] = dot(grad_scores, q, 0, 0)
                part_v[:, at] = dot(query_scores, g, 0, 0)

    def stage_c(m):
        for d in range(1, NY):
            y_in(m, d, True).wait_recv()

        @pl.loop(0, HC)
        def _(i):
            rows = pl.ds(pl.multiple_of(i * DH, DH), DH)
            totals = []
            for kind in range(2):
                total = got[m, 0, kind, rows, :].astype(F32)
                for j in range(1, NY):
                    total += got[m, j, kind, rows, :].astype(F32)
                totals.append(total)
            own_total[m, rows, :] = jnp.where(forward, totals[0], totals[1])
            core_out[m, rows, :] = jnp.where(forward, totals[1], totals[0])

        core_in(m).start()

    def stage_d(m):
        core_in(m).wait_recv()
        for i in range(NX):
            rows = slice(i * RX, (i + 1) * RX)
            x_out[m, i] = own_total[m, rows, :] + other_total[m, rows, :]
        for d in range(1, NX):
            x_in_copy(m, d).start()
        x_in[m, x] = x_out[m, x]

    def stage_e(m):
        for d in range(1, NX):
            x_in_copy(m, d, True).wait_recv()
        total = x_in[m, 0]
        for i in range(1, NX):
            total += x_in[m, i]
        z_buf[m, rank] = total.astype(BF16)
        for d in range(1, NZ):

            @pl.when(rank + d < NZ)
            def _():
                z_copy(m, d).start()

    def stage_z(m):
        z_sum[m] = jnp.zeros((RX, DH), F32)
        for d in range(1, NZ):

            @pl.when(rank - d >= 0)
            def _():
                z_copy(m, d, True).wait_recv()
                z_sum[m] += z_buf[m, rank - d].astype(F32)

        before = z_sum[m]
        ahead = [before]
        behind = [before]
        for i in range(NX - 1):
            ahead.append(ahead[-1] + x_in[m, i])
            behind.append(behind[-1] + x_in[m, NX - 1 - i])
        for i in range(NX):
            x_back[m, i] = jnp.where(forward, ahead[i], behind[NX - 1 - i])
        for d in range(1, NX):
            x_out_copy(m, d).start()
        base[m, x] = x_back[m, x]

    def stage_f(m):
        for d in range(1, NX):
            x_out_copy(m, d, True).wait_recv()
        for i in range(NX):
            rows = slice(i * RX, (i + 1) * RX)
            base_out[m, rows, :] = base[m, i] + own_total[m, rows, :]
        core_out_copy(m).start()

    def stage_g(m):
        core_out_copy(m).wait_recv()
        for i in range(NX):
            rows = slice(i * RX, (i + 1) * RX)
            mine = base[m, i]
            theirs = base_other[m, rows, :]
            run = jnp.where(forward, mine, theirs)
            for j in range(NY):
                y_out[m, j, 0, rows, :] = run.astype(BF16)
                if j < NY - 1:
                    run += got[m, j, 0, rows, :].astype(F32)
            run = jnp.where(forward, theirs, mine)
            for j in range(NY - 1, -1, -1):
                y_out[m, j, 1, rows, :] = run.astype(BF16)
                if j:
                    run += got[m, j, 1, rows, :].astype(F32)
        for d in (2, 1, 3):
            y_out_copy(m, d).start()
        final[m, y] = y_out[m, y]

    def stage_h(m):
        for d in range(1, NY):
            y_out_copy(m, d, True).wait_recv()

        @pl.loop(0, NY * HC // UNROLL)
        def _(n):
            for u in range(UNROLL):
                owner, i = (n * UNROLL + u) // HC, lax.rem(n * UNROLL + u, HC)
                at = lanes(m, owner, i)
                rows = pl.ds(pl.multiple_of(i * DH, DH), DH)
                prefix = final[m, owner, 0, rows, :]
                suffix = final[m, owner, 1, rows, :]
                oq_ref[:, at] = (part_q[:, at] + dot(g_ref[:, at], prefix, 1, 1)).astype(BF16)
                ok_ref[:, at] = (part_k[:, at] + dot(v_ref[:, at], suffix, 1, 1)).astype(BF16)
                ov_ref[:, at] = (part_v[:, at] + dot(k_ref[:, at], suffix, 1, 0)).astype(BF16)


    steps = []
    for m in range(M):
        arrives = Y_TIME * (m + 1) / M
        after = ((stage_c, 0), (stage_d, 1.2), (stage_e, 4.2), (stage_z, 9.5), (stage_f, 13), (stage_g, 14))
        steps += [(arrives + SPREAD * t, m, stage) for stage, t in after]
        steps.append((arrives + 23, m, stage_h))
        steps.append((2.0 + 2.5 * m, m, inside))
    pl.semaphore_wait(barrier, len(partners))
    for m in range(M):
        states(m)
    for _, m, stage in sorted(steps, key=lambda step: step[:2]):
        stage(m)
    for m in range(M):
        for d in range(1, NY):
            y_in(m, d).wait_send()
            y_out_copy(m, d).wait_send()
        for d in range(1, NX):
            x_in_copy(m, d).wait_send()
            x_out_copy(m, d).wait_send()
        for d in range(1, NZ):

            @pl.when(rank + d < NZ)
            def _():
                z_copy(m, d).wait_send()

        core_in(m).wait_send()
        core_out_copy(m).wait_send()


def finish(*refs):
    sources, targets, sem = refs[:3], refs[3:6], refs[6]
    copies = [pltpu.make_async_copy(a, b, sem.at[n]) for n, (a, b) in enumerate(zip(sources, targets))]
    for one in copies:
        one.start()
    for one in copies:
        one.wait()


def shards(queries, keys, values, grad_out):
    tokens = queries.shape[0]
    whole = pl.BlockSpec(memory_space=pl.ANY)
    dma = pltpu.SemaphoreType.DMA
    shapes = [jax.ShapeDtypeStruct((tokens, H * DH), BF16)] * 3
    results = pl.pallas_call(
        kernel,
        out_shape=shapes,
        in_specs=[whole] * 4,
        out_specs=[pl.BlockSpec(memory_space=pltpu.VMEM)] * 3,
        scratch_shapes=[pltpu.VMEM((tokens, H * DH), BF16)] * 4
        + [
            pltpu.VMEM((M, NY, 2, R, DH), BF16),
            pltpu.VMEM((M, NY, 2, R, DH), BF16),
            pltpu.VMEM((M, R, DH), F32),
            pltpu.VMEM((M, R, DH), F32),
            pltpu.VMEM((M, R, DH), F32),
            pltpu.VMEM((M, NX, RX, DH), F32),
            pltpu.VMEM((M, NX, RX, DH), F32),
            pltpu.VMEM((M, NZ, RX, DH), BF16),
            pltpu.VMEM((M, RX, DH), F32),
            pltpu.VMEM((M, NX, RX, DH), F32),
            pltpu.VMEM((M, NX, RX, DH), F32),
            pltpu.VMEM((M, R, DH), F32),
            pltpu.VMEM((M, R, DH), F32),
            pltpu.VMEM((M, NY, 2, R, DH), BF16),
            pltpu.VMEM((M, NY, 2, R, DH), BF16),
            pltpu.VMEM((tokens, H * DH), F32),
            pltpu.VMEM((tokens, H * DH), F32),
            pltpu.VMEM((tokens, H * DH), F32),
            dma((M, 4)),
            dma((M, NY)), dma((M, NY)),
            dma((M,)), dma((M,)),
            dma((M, NX)), dma((M, NX)),
            dma((M, NZ)), dma((M, NZ)),
            dma((M, NX)), dma((M, NX)),
            dma((M,)), dma((M,)),
            dma((M, NY)), dma((M, NY)),
        ],
        compiler_params=pltpu.CompilerParams(
            collective_id=0, has_side_effects=True, vmem_limit_bytes=VMEM_MIB * 2**20
        ),
        cost_estimate=pl.CostEstimate(
            flops=20 * DH**3 * H, bytes_accessed=14 * tokens * H * DH, transcendentals=0
        ),
        name="scan",
    )(queries, keys, values, grad_out)
    return pl.pallas_call(
        finish,
        out_shape=shapes,
        in_specs=[pl.BlockSpec(memory_space=pltpu.VMEM)] * 3,
        out_specs=[whole] * 3,
        scratch_shapes=[dma((3,))],
        cost_estimate=pl.CostEstimate(flops=0, bytes_accessed=12 * tokens * H * DH, transcendentals=0),
        compiler_params=pltpu.CompilerParams(vmem_limit_bytes=8 * 2**20),
        name="finish",
    )(*results)


def solution(mesh):
    spec = P(("seq", "head"), None)
    return jax.shard_map(
        shards, mesh=mesh, in_specs=(spec,) * 4, out_specs=(spec,) * 3, check_vma=False
    )
```

```python
import jax
import jax.numpy as jnp
from jax import lax
from jax.experimental import pallas as pl
from jax.experimental.pallas import tpu as pltpu
from jax.sharding import PartitionSpec as P

H = 32
DH = 128
NZ, NX, NY = 8, 4, 4
PER = H // NY
M = 4
HC = PER // M
WIDE = NY * HC * DH
R = HC * DH
RX = R // NX
UNROLL = 8
VMEM_MIB = 50
SPREAD = 1.0
Y_TIME = 23.0
MESH = pl.DeviceIdType.MESH
F32 = jnp.float32
BF16 = jnp.bfloat16


def dot(left, right, left_dim, right_dim):
    return lax.dot_general(
        left, right, (((left_dim,), (right_dim,)), ((), ())), preferred_element_type=F32
    )


def kernel(
    q_hbm, k_hbm, v_hbm, g_hbm, oq_ref, ok_ref, ov_ref,
    q_ref, k_ref, v_ref, g_ref, sent, got, own_total, other_total, core_out, x_out, x_in, z_buf, z_sum, x_back, base, base_out, base_other,
    y_out, final, part_q, part_k, part_v,
    in_sem, yi_s, yi_r, c1_s, c1_r, xi_s, xi_r, zz_s, zz_r, xo_s, xo_r, c2_s, c2_r, yo_s, yo_r,
):
    s = lax.axis_index("seq")
    y = lax.axis_index("head")
    c = lax.rem(s, 2)
    x = lax.rem(s // 2, NX)
    z = s // (2 * NX)
    forward = c == 0
    mate = (s + 1 - 2 * c, y)
    rank = jnp.where(forward, z, NZ - 1 - z)

    def at_y(d):
        return lax.rem(y + d, NY)

    def at_x(d):
        return lax.rem(x + d, NX)

    def x_dev(i):
        return ((z * NX + i) * 2 + c, y)

    def z_dev(place):
        return ((jnp.where(forward, place, NZ - 1 - place) * NX + x) * 2 + c, y)

    def copy(src, dst, send, recv, device):
        return pltpu.make_async_remote_copy(
            src_ref=src, dst_ref=dst, send_sem=send, recv_sem=recv, device_id=device, device_id_type=MESH
        )

    barrier = pltpu.get_barrier_semaphore()
    partners = (
        [mate]
        + [(s, at_y(d)) for d in range(1, NY)]
        + [x_dev(at_x(d)) for d in range(1, NX)]
        + [z_dev(lax.rem(rank + d, NZ)) for d in range(1, NZ)]
    )
    for partner in partners:
        pl.semaphore_signal(barrier, inc=1, device_id=partner, device_id_type=MESH)

    def lanes(m, owner, i):
        return pl.ds(pl.multiple_of(((m * NY + owner) * HC + i) * DH, DH), DH)

    def load(m):
        columns = slice(m * WIDE, (m + 1) * WIDE)
        pairs = ((k_hbm, k_ref), (v_hbm, v_ref), (q_hbm, q_ref), (g_hbm, g_ref))
        return [
            pltpu.make_async_copy(a.at[:, columns], b.at[:, columns], in_sem.at[m, n])
            for n, (a, b) in enumerate(pairs)
        ]

    for m in range(M):
        for one in load(m):
            one.start()

    def y_in(m, d, receive=False):
        slot = at_y(NY - d) if receive else y
        return copy(sent.at[m, at_y(d)], got.at[m, slot], yi_s.at[m, d], yi_r.at[m, d], (s, at_y(d)))

    def core_in(m):
        return copy(core_out.at[m], other_total.at[m], c1_s.at[m], c1_r.at[m], mate)

    def x_in_copy(m, d, receive=False):
        slot = at_x(NX - d) if receive else x
        return copy(x_out.at[m, at_x(d)], x_in.at[m, slot], xi_s.at[m, d], xi_r.at[m, d], x_dev(at_x(d)))

    def z_copy(m, d, receive=False):
        slot = rank - d if receive else rank
        device = z_dev(lax.rem(rank + d, NZ))
        return copy(z_buf.at[m, rank], z_buf.at[m, slot], zz_s.at[m, d], zz_r.at[m, d], device)

    def x_out_copy(m, d, receive=False):
        slot = at_x(NX - d) if receive else x
        return copy(x_back.at[m, at_x(d)], base.at[m, slot], xo_s.at[m, d], xo_r.at[m, d], x_dev(at_x(d)))

    def core_out_copy(m):
        return copy(base_out.at[m], base_other.at[m], c2_s.at[m], c2_r.at[m], mate)

    def y_out_copy(m, d, receive=False):
        slot = at_y(NY - d) if receive else y
        return copy(y_out.at[m, at_y(d)], final.at[m, slot], yo_s.at[m, d], yo_r.at[m, d], (s, at_y(d)))

    def states(m):
        for one in load(m):
            one.wait()
        for d in (2, 1, 3, 0):
            owner = at_y(d)
            for i in range(HC):
                at = lanes(m, owner, i)
                rows = slice(i * DH, (i + 1) * DH)
                key_state = dot(k_ref[:, at], v_ref[:, at], 0, 0).astype(BF16)
                grad_state = dot(q_ref[:, at], g_ref[:, at], 0, 0).astype(BF16)
                if d:
                    sent[m, owner, 0, rows, :] = key_state
                    sent[m, owner, 1, rows, :] = grad_state
                else:
                    got[m, y, 0, rows, :] = key_state
                    got[m, y, 1, rows, :] = grad_state
            if d:
                y_in(m, d).start()

    def inside(m):
        row = lax.broadcasted_iota(jnp.int32, (DH, DH), 0)
        column = lax.broadcasted_iota(jnp.int32, (DH, DH), 1)
        causal = column <= row

        @pl.loop(0, NY * HC // UNROLL)
        def _(n):
            for u in range(UNROLL):
                at = lanes(m, 0, n * UNROLL + u)
                q, k, v, g = q_ref[:, at], k_ref[:, at], v_ref[:, at], g_ref[:, at]
                grad_scores = jnp.where(causal, dot(g, v, 1, 1), 0.0).astype(BF16)
                query_scores = jnp.where(causal, dot(q, k, 1, 1), 0.0).astype(BF16)
                part_q[:, at] = dot(grad_scores, k, 1, 0)
                part_k[:, at] = dot(grad_scores, q, 0, 0)
                part_v[:, at] = dot(query_scores, g, 0, 0)

    def stage_c(m):
        for d in range(1, NY):
            y_in(m, d, True).wait_recv()

        @pl.loop(0, HC)
        def _(i):
            rows = pl.ds(pl.multiple_of(i * DH, DH), DH)
            totals = []
            for kind in range(2):
                total = got[m, 0, kind, rows, :].astype(F32)
                for j in range(1, NY):
                    total += got[m, j, kind, rows, :].astype(F32)
                totals.append(total)
            own_total[m, rows, :] = jnp.where(forward, totals[0], totals[1])
            core_out[m, rows, :] = jnp.where(forward, totals[1], totals[0])

        core_in(m).start()

    def stage_d(m):
        core_in(m).wait_recv()
        for i in range(NX):
            rows = slice(i * RX, (i + 1) * RX)
            x_out[m, i] = own_total[m, rows, :] + other_total[m, rows, :]
        for d in range(1, NX):
            x_in_copy(m, d).start()
        x_in[m, x] = x_out[m, x]

    def stage_e(m):
        for d in range(1, NX):
            x_in_copy(m, d, True).wait_recv()
        total = x_in[m, 0]
        for i in range(1, NX):
            total += x_in[m, i]
        z_buf[m, rank] = total.astype(BF16)
        for d in range(1, NZ):

            @pl.when(rank + d < NZ)
            def _():
                z_copy(m, d).start()

    def stage_z(m):
        z_sum[m] = jnp.zeros((RX, DH), F32)
        for d in range(1, NZ):

            @pl.when(rank - d >= 0)
            def _():
                z_copy(m, d, True).wait_recv()
                z_sum[m] += z_buf[m, rank - d].astype(F32)

        before = z_sum[m]
        ahead = [before]
        behind = [before]
        for i in range(NX - 1):
            ahead.append(ahead[-1] + x_in[m, i])
            behind.append(behind[-1] + x_in[m, NX - 1 - i])
        for i in range(NX):
            x_back[m, i] = jnp.where(forward, ahead[i], behind[NX - 1 - i])
        for d in range(1, NX):
            x_out_copy(m, d).start()
        base[m, x] = x_back[m, x]

    def stage_f(m):
        for d in range(1, NX):
            x_out_copy(m, d, True).wait_recv()
        for i in range(NX):
            rows = slice(i * RX, (i + 1) * RX)
            base_out[m, rows, :] = base[m, i] + own_total[m, rows, :]
        core_out_copy(m).start()

    def stage_g(m):
        core_out_copy(m).wait_recv()
        for i in range(NX):
            rows = slice(i * RX, (i + 1) * RX)
            mine = base[m, i]
            theirs = base_other[m, rows, :]
            run = jnp.where(forward, mine, theirs)
            for j in range(NY):
                y_out[m, j, 0, rows, :] = run.astype(BF16)
                if j < NY - 1:
                    run += got[m, j, 0, rows, :].astype(F32)
            run = jnp.where(forward, theirs, mine)
            for j in range(NY - 1, -1, -1):
                y_out[m, j, 1, rows, :] = run.astype(BF16)
                if j:
                    run += got[m, j, 1, rows, :].astype(F32)
        for d in (2, 1, 3):
            y_out_copy(m, d).start()
        final[m, y] = y_out[m, y]

    def stage_h(m):
        for d in range(1, NY):
            y_out_copy(m, d, True).wait_recv()

        @pl.loop(0, NY * HC // UNROLL)
        def _(n):
            for u in range(UNROLL):
                owner, i = (n * UNROLL + u) // HC, lax.rem(n * UNROLL + u, HC)
                at = lanes(m, owner, i)
                rows = pl.ds(pl.multiple_of(i * DH, DH), DH)
                prefix = final[m, owner, 0, rows, :]
                suffix = final[m, owner, 1, rows, :]
                oq_ref[:, at] = (part_q[:, at] + dot(g_ref[:, at], prefix, 1, 1)).astype(BF16)
                ok_ref[:, at] = (part_k[:, at] + dot(v_ref[:, at], suffix, 1, 1)).astype(BF16)
                ov_ref[:, at] = (part_v[:, at] + dot(k_ref[:, at], suffix, 1, 0)).astype(BF16)


    steps = []
    for m in range(M):
        arrives = Y_TIME * (m + 1) / M
        after = ((stage_c, 0), (stage_d, 1.2), (stage_e, 4.2), (stage_z, 9.5), (stage_f, 13), (stage_g, 14))
        steps += [(arrives + SPREAD * t, m, stage) for stage, t in after]
        steps.append((arrives + 23, m, stage_h))
        steps.append((2.0 + 2.5 * m, m, inside))
    pl.semaphore_wait(barrier, len(partners))
    for m in range(M):
        states(m)
    for _, m, stage in sorted(steps, key=lambda step: step[:2]):
        stage(m)
    for m in range(M):
        for d in range(1, NY):
            y_in(m, d).wait_send()
            y_out_copy(m, d).wait_send()
        for d in range(1, NX):
            x_in_copy(m, d).wait_send()
            x_out_copy(m, d).wait_send()
        for d in range(1, NZ):

            @pl.when(rank + d < NZ)
            def _():
                z_copy(m, d).wait_send()

        core_in(m).wait_send()
        core_out_copy(m).wait_send()


def finish(*refs):
    sources, targets, sem = refs[:3], refs[3:6], refs[6]
    copies = [pltpu.make_async_copy(a, b, sem.at[n]) for n, (a, b) in enumerate(zip(sources, targets))]
    for one in copies:
        one.start()
    for one in copies:
        one.wait()


def shards(queries, keys, values, grad_out):
    tokens = queries.shape[0]
    whole = pl.BlockSpec(memory_space=pl.ANY)
    dma = pltpu.SemaphoreType.DMA
    shapes = [jax.ShapeDtypeStruct((tokens, H * DH), BF16)] * 3
    results = pl.pallas_call(
        kernel,
        out_shape=shapes,
        in_specs=[whole] * 4,
        out_specs=[pl.BlockSpec(memory_space=pltpu.VMEM)] * 3,
        scratch_shapes=[pltpu.VMEM((tokens, H * DH), BF16)] * 4
        + [
            pltpu.VMEM((M, NY, 2, R, DH), BF16),
            pltpu.VMEM((M, NY, 2, R, DH), BF16),
            pltpu.VMEM((M, R, DH), F32),
            pltpu.VMEM((M, R, DH), F32),
            pltpu.VMEM((M, R, DH), F32),
            pltpu.VMEM((M, NX, RX, DH), F32),
            pltpu.VMEM((M, NX, RX, DH), F32),
            pltpu.VMEM((M, NZ, RX, DH), BF16),
            pltpu.VMEM((M, RX, DH), F32),
            pltpu.VMEM((M, NX, RX, DH), F32),
            pltpu.VMEM((M, NX, RX, DH), F32),
            pltpu.VMEM((M, R, DH), F32),
            pltpu.VMEM((M, R, DH), F32),
            pltpu.VMEM((M, NY, 2, R, DH), BF16),
            pltpu.VMEM((M, NY, 2, R, DH), BF16),
            pltpu.VMEM((tokens, H * DH), F32),
            pltpu.VMEM((tokens, H * DH), F32),
            pltpu.VMEM((tokens, H * DH), F32),
            dma((M, 4)),
            dma((M, NY)), dma((M, NY)),
            dma((M,)), dma((M,)),
            dma((M, NX)), dma((M, NX)),
            dma((M, NZ)), dma((M, NZ)),
            dma((M, NX)), dma((M, NX)),
            dma((M,)), dma((M,)),
            dma((M, NY)), dma((M, NY)),
        ],
        compiler_params=pltpu.CompilerParams(
            collective_id=0, has_side_effects=True, vmem_limit_bytes=VMEM_MIB * 2**20
        ),
        cost_estimate=pl.CostEstimate(
            flops=20 * DH**3 * H, bytes_accessed=14 * tokens * H * DH, transcendentals=0
        ),
        name="scan",
    )(queries, keys, values, grad_out)
    return pl.pallas_call(
        finish,
        out_shape=shapes,
        in_specs=[pl.BlockSpec(memory_space=pltpu.VMEM)] * 3,
        out_specs=[whole] * 3,
        scratch_shapes=[dma((3,))],
        cost_estimate=pl.CostEstimate(flops=0, bytes_accessed=12 * tokens * H * DH, transcendentals=0),
        compiler_params=pltpu.CompilerParams(vmem_limit_bytes=8 * 2**20),
        name="finish",
    )(*results)


def solution(mesh):
    spec = P(("seq", "head"), None)
    return jax.shard_map(
        shards, mesh=mesh, in_specs=(spec,) * 4, out_specs=(spec,) * 3, check_vma=False
    )
```
